32 devices in a mesh: dp: 8 (over y, x, core), tensor: 4 (over z).
Axes of the slice: x: 2, y: 2, z: 4, core: 2. Of those that a mesh axis runs over, the one named last changes fastest.
Arguments:
- inputs: bfloat16 [24576, 2048], P(('dp', 'tensor')), may hold values from -6 to 6
- seq_offsets: int32 [8, 3], P('dp'), may hold values from 0 to 3072, as said below
- seq_lengths: int32 [8, 3], P('dp'), may hold values from 0 to 3072, as said below
- norm1_gain: float32 [2048], replicated, may hold values from 0.5 to 1.5
- w_qkv: float32 [2048, 3, 2048], P('dp', None, 'tensor'), may hold values from -0.125 to 0.125
- w_gate_out: float32 [2048, 2048], P('dp', 'tensor'), may hold values from -0.125 to 0.125
- w_decay: float32 [2048, 2, 16], P('dp', None, 'tensor'), may hold values from -0.125 to 0.125
- conv_weight: float32 [3, 4, 2048], P(None, None, 'tensor'), may hold values from -3 to 3
- decay_log: float32 [16], P('tensor'), may hold values from -2 to 1
- decay_bias: float32 [16], P('tensor'), may hold values from -10 to -3
- head_norm_gain: float32 [128], replicated, may hold values from 0.5 to 1.5
- w_output: float32 [2048, 2048], P('dp', 'tensor'), may hold values from -0.125 to 0.125
- norm2_gain: float32 [2048], replicated, may hold values from 0.5 to 1.5
- w_mlp_in: float32 [2048, 2, 5632], P('dp', None, 'tensor'), may hold values from -0.125 to 0.125
- w_mlp_out: float32 [2048, 5632], P('dp', 'tensor'), may hold values from -0.078125 to 0.078125
- cotangent: bfloat16 [24576, 2048], P(('dp', 'tensor')), may hold values from -6 to 6
Outputs:
- output: bfloat16 [24576, 2048], P(('dp', 'tensor'))
- grad_inputs: float32 [24576, 2048], P(('dp', 'tensor'))
- grad_norm1_gain: float32 [2048], replicated
- grad_w_qkv: float32 [2048, 3, 2048], P('dp', None, 'tensor')
- grad_w_gate_out: float32 [2048, 2048], P('dp', 'tensor')
- grad_w_decay: float32 [2048, 2, 16], P('dp', None, 'tensor')
- grad_conv_weight: float32 [3, 4, 2048], P(None, None, 'tensor')
- grad_decay_log: float32 [16], P('tensor')
- grad_decay_bias: float32 [16], P('tensor')
- grad_head_norm_gain: float32 [128], replicated
- grad_w_output: float32 [2048, 2048], P('dp', 'tensor')
- grad_norm2_gain: float32 [2048], replicated
- grad_w_mlp_in: float32 [2048, 2, 5632], P('dp', None, 'tensor')
- grad_w_mlp_out: float32 [2048, 5632], P('dp', 'tensor')
The draws below stay inside these ranges and needn't reach their ends.
Inputs may be any that keep to these rules, and one draw needn't show every extreme that they name: `seq_offsets`: offsets and lengths are multiples of 64. In each group the used slots come first (at least one), each of 1024 tokens or more; the sequences lie in slot order without intersection, possibly with unused rows between them, and end by 3072; an unused slot has length 0 and offset 3072. In every draw some group holds one sequence that fills it completely. `seq_lengths`: see seq_offsets.
All inputs are finite; a program needn't handle non-finite values.
Results may differ from the reference program's by a relative error of at most 0.02.
The reference program's roundings to bfloat16 on the way count: a program that leaves them out, or rounds other values in their place, can miss the bound.
Values may be sent and summed in bfloat16 or wider, within the bound.
A program may use at most 640 MiB of HBM per device.

```python
import jax
import jax.numpy as jnp
from jax import lax

D = 2048
HEADS = 16
HEAD_DIM = 128
FF = 5632
BLOCK = 64
MIN_LEN = 1024
SLOTS = 3
CAP = 3072
TOKENS = 24576
N_DP = 8
N_TENSOR = 4


def layout(key):
    count_key, full_key, used_key, share_key, gap_key = jax.random.split(key, 5)
    min_blocks = MIN_LEN // BLOCK
    cap_blocks = CAP // BLOCK
    group_index = jnp.arange(N_DP, dtype=jnp.int32)
    full_group = jax.random.randint(full_key, (), 0, N_DP)
    counts = jax.random.randint(count_key, (N_DP,), 1, SLOTS + 1)
    counts = jnp.where(group_index == full_group, 1, counts)
    slot_index = jnp.arange(SLOTS, dtype=jnp.int32)[None, :]
    active = (slot_index < counts[:, None]).astype(jnp.int32)
    spare_blocks = cap_blocks - counts * min_blocks
    used_blocks = jax.random.randint(used_key, (N_DP,), 0, spare_blocks + 1)
    used_blocks = jnp.where(group_index == full_group, spare_blocks, used_blocks)
    shares = jax.random.randint(share_key, (N_DP, SLOTS), 1, 9) * active
    extra_blocks = used_blocks[:, None] * shares // jnp.sum(shares, axis=1, keepdims=True)
    extra_blocks = extra_blocks + (slot_index == 0).astype(jnp.int32) * (used_blocks - jnp.sum(extra_blocks, axis=1))[:, None]
    lengths = (min_blocks + extra_blocks) * active
    gap_total = cap_blocks - jnp.sum(lengths, axis=1)
    gap_weights = jax.random.randint(gap_key, (N_DP, SLOTS), 0, 9) * active
    gap_blocks = gap_total[:, None] * gap_weights // (jnp.sum(gap_weights, axis=1, keepdims=True) + 1)
    offsets = jnp.cumsum(gap_blocks + lengths, axis=1) - lengths
    offsets = jnp.where(active > 0, offsets, cap_blocks)
    return ((offsets * BLOCK).astype(jnp.int32), (lengths * BLOCK).astype(jnp.int32))


def draw_seq_offsets(key, part):
    shared = layout(key)
    return shared[0]


def draw_seq_lengths(key, part):
    shared = layout(key)
    return shared[1]


def block_scale(own_key, shape, pieces, smallest, high):
    gain, own = 1.0, jax.random.fold_in(own_key, 6)
    for axis_at, blocks in pieces:
        draws = jnp.exp(jax.random.uniform(jax.random.fold_in(own, axis_at), (blocks,), jnp.float32, smallest / len(pieces), high / len(pieces)))
        gain = gain * jnp.repeat(draws, shape[axis_at] // blocks).reshape([-1 if axis == axis_at else 1 for axis in range(len(shape))])
    return gain


def centred(own_key, shape, scale, limit, shards=(), held_as=jnp.bfloat16):
    level = block_scale(own_key, shape, shards, -0.22, 0.18) if shards else 1.0
    drawn = jax.random.normal(own_key, shape, jnp.float32) * scale * level
    return jnp.minimum(jnp.maximum(drawn, -limit), limit).astype(held_as)


def setup_inputs(seed: int = 0) -> dict:
    seeds = jax.random.split(jax.random.key(seed), 17)
    return {
        "inputs": centred(seeds[0], (TOKENS, D), 1.0, 6.0, ((0, 32),)),
        "seq_offsets": draw_seq_offsets(jax.random.fold_in(seeds[16], 71), 0),
        "seq_lengths": draw_seq_lengths(jax.random.fold_in(seeds[16], 71), 0),
        "norm1_gain": jnp.clip(1.0 + 0.1 * jax.random.normal(seeds[3], (D,), jnp.float32), 0.5, 1.5),
        "w_qkv": centred(seeds[4], (D, 3, D), D ** -0.5, 0.125, ((0, 8), (2, 4)), jnp.float32),
        "w_gate_out": centred(seeds[5], (D, D), D ** -0.5, 0.125, ((0, 8), (1, 4)), jnp.float32),
        "w_decay": centred(seeds[6], (D, 2, HEADS), D ** -0.5, 0.125, ((0, 8), (2, 4)), jnp.float32),
        "conv_weight": centred(seeds[7], (3, 4, D), 0.5, 3.0, ((2, 4),), jnp.float32),
        "decay_log": jnp.clip(-2.0 + 3.0 * jax.random.uniform(seeds[8], (HEADS,), jnp.float32) ** block_scale(seeds[8], (HEADS,), ((0, 4),), -0.2, 0.2), -2.0, 1.0),
        "decay_bias": jnp.clip(-10.0 + 7.0 * jax.random.uniform(seeds[9], (HEADS,), jnp.float32) ** block_scale(seeds[9], (HEADS,), ((0, 4),), -0.2, 0.2), -10.0, -3.0),
        "head_norm_gain": jnp.clip(1.0 + 0.1 * jax.random.normal(seeds[10], (HEAD_DIM,), jnp.float32), 0.5, 1.5),
        "w_output": centred(seeds[11], (D, D), D ** -0.5, 0.125, ((0, 8), (1, 4)), jnp.float32),
        "norm2_gain": jnp.clip(1.0 + 0.1 * jax.random.normal(seeds[12], (D,), jnp.float32), 0.5, 1.5),
        "w_mlp_in": centred(seeds[13], (D, 2, FF), D ** -0.5, 0.125, ((0, 8), (2, 4)), jnp.float32),
        "w_mlp_out": centred(seeds[14], (D, FF), FF ** -0.5, 0.078125, ((0, 8), (1, 4)), jnp.float32),
        "cotangent": centred(seeds[15], (TOKENS, D), 1.0, 6.0, ((0, 32),)),
    }


epsilon = 1e-06
top_precision = lax.Precision.HIGHEST

@jax.custom_vjp
def low(v):
    return lax.optimization_barrier(v.astype(jnp.bfloat16)).astype(jnp.float32)

@jax.custom_vjp
def low_back(v):
    return v

def low_keep(v):
    return (low(v), None)

def low_pass(kept, grad):
    return (grad,)

def back_keep(v):
    return (v, None)

def back_low(kept, grad):
    return (low(grad),)
low.defvjp(low_keep, low_pass)
low_back.defvjp(back_keep, back_low)

def segment_info(offsets, lengths, total):
    positions = jnp.arange(total, dtype=jnp.int32)[:, None]
    inside = (positions >= offsets[None, :]) & (positions < offsets[None, :] + lengths[None, :])
    live_rows = jnp.any(inside, axis=1)
    place = lax.optimization_barrier(jnp.sum(jnp.where(inside, positions - offsets[None, :], 0), axis=1))
    taps = jnp.arange(4, dtype=jnp.int32)
    tap_mask = place[:, None] >= 3 - taps[None, :]
    starts = jnp.arange(total // BLOCK, dtype=jnp.int32) * BLOCK
    resets = jnp.any((starts[:, None] == offsets[None, :]) & (lengths[None, :] > 0), axis=1)
    return (live_rows, tap_mask, resets)

def short_conv(values, kernel, tap_mask):
    total = values.shape[0]
    padded = jnp.pad(values, ((3, 0), (0, 0), (0, 0)))
    result = jnp.zeros_like(values)
    for kernel_tap in range(4):
        term = kernel[:, kernel_tap, :][None] * padded[kernel_tap:kernel_tap + total]
        result = result + jnp.where(tap_mask[:, kernel_tap][:, None, None], term, 0.0)
    return result

def block_step(recurrent_state, block_data):
    query_rows, key_matrix_rows, values, decays, beta_gate, restart = block_data
    recurrent_state = jnp.where(restart, 0.0, recurrent_state)
    width = decays.shape[1]
    head_dimension = key_matrix_rows.shape[2]
    running_total = jnp.cumsum(decays, axis=1)
    strict_lower = jnp.tril(jnp.ones((width, width), dtype=bool), -1)
    lower_incl = jnp.tril(jnp.ones((width, width), dtype=bool))
    spread = running_total[:, :, None] - running_total[:, None, :]
    strict_decay = jnp.where(strict_lower, jnp.exp(jnp.where(strict_lower, spread, 0.0)), 0.0)
    incl_decay = jnp.where(lower_incl, jnp.exp(jnp.where(lower_incl, spread, 0.0)), 0.0)
    key_inner = jnp.einsum('hik,hjk->hij', key_matrix_rows, key_matrix_rows, precision=top_precision)
    system = jnp.eye(width, dtype=decays.dtype) + beta_gate[:, :, None] * key_inner * strict_decay
    right_side = jnp.concatenate([key_matrix_rows * (beta_gate * jnp.exp(running_total))[:, :, None], values * beta_gate[:, :, None]], axis=2)
    triangular_answer = jax.scipy.linalg.solve_triangular(system, right_side, lower=True, unit_diagonal=True)
    newest_value = triangular_answer[:, :, head_dimension:] - jnp.einsum('wrq,wqm->wrm', triangular_answer[:, :, :head_dimension], recurrent_state, precision=top_precision)
    scores = jnp.einsum('hik,hjk->hij', query_rows, key_matrix_rows, precision=top_precision) * incl_decay
    output_rows = jnp.einsum('wrq,wqm->wrm', query_rows * jnp.exp(running_total)[:, :, None], recurrent_state, precision=top_precision)
    output_rows = output_rows + jnp.einsum('hij,hjv->hiv', scores, newest_value, precision=top_precision)
    trailing_part = jnp.exp(running_total[:, -1:] - running_total)
    recurrent_state = jnp.exp(running_total[:, -1])[:, None, None] * recurrent_state + jnp.einsum('atf,atz->afz', key_matrix_rows * trailing_part[:, :, None], newest_value, precision=top_precision)
    return (recurrent_state, output_rows)

def mixer_local(z_qkv, z_gate, z_decay, kernel, decay_log, decay_bias, head_gain, tap_mask, resets):
    total = z_qkv.shape[0]
    heads = decay_log.shape[0]
    blocks = total // BLOCK
    mixed = jax.nn.silu(short_conv(z_qkv, kernel, tap_mask))
    query_rows = mixed[:, 0].reshape(total, heads, HEAD_DIM)
    key_matrix_rows = mixed[:, 1].reshape(total, heads, HEAD_DIM)
    values = mixed[:, 2].reshape(total, heads, HEAD_DIM)
    query_rows = query_rows * lax.rsqrt(lax.optimization_barrier(jnp.sum(query_rows * query_rows, axis=-1, keepdims=True)) + epsilon) * HEAD_DIM ** (-0.5)
    key_matrix_rows = key_matrix_rows * lax.rsqrt(lax.optimization_barrier(jnp.sum(key_matrix_rows * key_matrix_rows, axis=-1, keepdims=True)) + epsilon)
    decays = -jnp.exp(decay_log) * jax.nn.softplus(z_decay[:, 0] + decay_bias)
    beta_gate = jax.nn.sigmoid(z_decay[:, 1])

    def to_blocks(array):
        return jnp.swapaxes(array.reshape((blocks, BLOCK) + array.shape[1:]), 1, 2)
    start_memory = jnp.zeros((heads, HEAD_DIM, HEAD_DIM), dtype=query_rows.dtype)
    block_inputs = (to_blocks(query_rows), to_blocks(key_matrix_rows), to_blocks(values), to_blocks(decays), to_blocks(beta_gate), resets)
    _, output_rows = lax.scan(jax.checkpoint(block_step), start_memory, block_inputs)
    output_rows = jnp.swapaxes(output_rows, 1, 2).reshape(total, heads, HEAD_DIM)
    normed = output_rows * lax.rsqrt(lax.optimization_barrier(jnp.mean(output_rows * output_rows, axis=-1, keepdims=True)) + epsilon) * head_gain
    return normed.reshape(total, heads * HEAD_DIM) * jax.nn.silu(z_gate)

def reference(inputs, seq_offsets, seq_lengths, norm1_gain, w_qkv, w_gate_out, w_decay, conv_weight, decay_log, decay_bias, head_norm_gain, w_output, norm2_gain, w_mlp_in, w_mlp_out, cotangent):
    local_width = D // N_TENSOR
    local_heads = HEADS // N_TENSOR
    local_hidden = FF // N_TENSOR
    stream = inputs.astype(jnp.float32).reshape(N_DP, CAP, D)
    params = (norm1_gain, w_qkv, w_gate_out, w_decay, conv_weight, decay_log, decay_bias, head_norm_gain, w_output, norm2_gain, w_mlp_in, w_mlp_out)

    def forward(stream_in, param_set):
        gain_first, qkv_full, gate_full, decay_full, kernel, log_rate, rate_bias, head_gain, out_full, gain_second, mlp_in_full, mlp_out_full = param_set
        qkv_low = low(qkv_full).reshape(D, 3, N_TENSOR, local_width)
        gate_low = low(gate_full).reshape(D, N_TENSOR, local_width)
        decay_low = low(decay_full).reshape(D, 2, N_TENSOR, local_heads)
        out_low = low(out_full).reshape(D, N_TENSOR, local_width)
        mlp_in_low = low(mlp_in_full).reshape(D, 2, N_TENSOR, local_hidden)
        mlp_out_low = low(mlp_out_full).reshape(D, N_TENSOR, local_hidden)

        def group_fn(carry, item):
            rows_in, offsets, lengths = item
            live_rows, tap_mask, resets = segment_info(offsets, lengths, CAP)
            scale_first = lax.rsqrt(lax.optimization_barrier(jnp.mean(rows_in * rows_in, axis=-1, keepdims=True)) + epsilon)
            normed_first = low(rows_in * scale_first * gain_first)
            copies = low_back(jnp.broadcast_to(normed_first, (N_TENSOR, CAP, D)))
            z_qkv = low_back(jnp.einsum('gcd,dsgk->csgk', copies, qkv_low, precision=top_precision)).reshape(CAP, 3, D)
            z_gate = low_back(jnp.einsum('gcd,dgk->cgk', copies, gate_low, precision=top_precision)).reshape(CAP, D)
            z_decay = low_back(jnp.einsum('gcd,dsgh->csgh', copies, decay_low, precision=top_precision)).reshape(CAP, 2, HEADS)
            gated = low(mixer_local(z_qkv, z_gate, z_decay, kernel, log_rate, rate_bias, head_gain, tap_mask, resets))
            parts = low(jnp.einsum('cgk,mgk->gcm', gated.reshape(CAP, N_TENSOR, local_width), out_low, precision=top_precision))
            middle = rows_in + low_back(lax.optimization_barrier(jnp.sum(parts, axis=0)))
            scale_second = lax.rsqrt(lax.optimization_barrier(jnp.mean(middle * middle, axis=-1, keepdims=True)) + epsilon)
            normed_second = low(middle * scale_second * gain_second)
            copies_second = low_back(jnp.broadcast_to(normed_second, (N_TENSOR, CAP, D)))
            z_mlp = low_back(jnp.einsum('gcd,dsgf->gcsf', copies_second, mlp_in_low, precision=top_precision))
            hidden = low(jax.nn.silu(z_mlp[:, :, 0]) * z_mlp[:, :, 1])
            feed_parts = low(jnp.einsum('gcf,mgf->gcm', hidden, mlp_out_low, precision=top_precision))
            result = live_rows.astype(jnp.float32)[:, None] * (middle + low_back(lax.optimization_barrier(jnp.sum(feed_parts, axis=0))))
            return (carry, result)
        _, results = lax.scan(jax.checkpoint(group_fn), None, (stream_in, seq_offsets, seq_lengths))
        return results
    result, backward = jax.vjp(forward, stream, params)
    grad_stream, grad_params = backward(cotangent.astype(jnp.float32).reshape(N_DP, CAP, D))
    return (result.reshape(TOKENS, D).astype(jnp.bfloat16), grad_stream.reshape(TOKENS, D), grad_params[0], grad_params[1], grad_params[2], grad_params[3], grad_params[4], grad_params[5], grad_params[6], grad_params[7], grad_params[8], grad_params[9], grad_params[10], grad_params[11])
```

```python
import functools

import jax
import jax.numpy as jnp
from jax import lax
from jax.experimental import pallas as pl
from jax.experimental.pallas import tpu as pltpu
from jax.sharding import PartitionSpec as P

HEAD_DIM = 128
BLOCK = 64
epsilon = 1e-06
top_precision = lax.Precision.HIGHEST

NN = ((1,), (0,))
NT = ((1,), (1,))
TN = ((0,), (0,))


def mm(a, b, dims=NN, passes=1):
    if passes == 6:
        return lax.dot_general(
            a, b, (dims, ((), ())), precision=top_precision, preferred_element_type=jnp.float32
        )
    ah, bh = a.astype(jnp.bfloat16), b.astype(jnp.bfloat16)
    dot = lambda x, y: lax.dot_general(
        x, y, (dims, ((), ())), preferred_element_type=jnp.float32
    )
    total = dot(ah, bh)
    if passes == 3:
        al = (a - ah.astype(jnp.float32)).astype(jnp.bfloat16)
        bl = (b - bh.astype(jnp.float32)).astype(jnp.bfloat16)
        total = total + (dot(al, bh) + dot(ah, bl))
    return total


PASS = dict(gram=3, inv=3, solve=3, state=3, out=3, back=3)


def sigmoid(v):
    return 1.0 / (1.0 + jnp.exp(-v))


def lane_sum(v):
    return jnp.sum(v, axis=-1, keepdims=True)


def block_flags(offsets_ref, lengths_ref, start):
    live = jnp.int32(0)
    fresh = jnp.int32(0)
    for slot in range(offsets_ref.shape[1]):
        first, size = offsets_ref[0, slot], lengths_ref[0, slot]
        live = live | ((start >= first) & (start < first + size)).astype(jnp.int32)
        fresh = fresh | ((start == first) & (size > 0)).astype(jnp.int32)
    return live, fresh


def as_scale(flag):
    return jnp.where(flag > 0, 1.0, 0.0).astype(jnp.float32)


def square_masks():
    row = lax.broadcasted_iota(jnp.int32, (BLOCK, BLOCK), 0)
    col = lax.broadcasted_iota(jnp.int32, (BLOCK, BLOCK), 1)
    return row, col


def conv_block(ext, taps, live):
    shifted = [ext[8:]] + [ext[8 - d : 8 - d + BLOCK] * live for d in (1, 2, 3)]
    total = taps[3:4] * shifted[0]
    for d in (1, 2, 3):
        total = total + taps[3 - d : 4 - d] * shifted[d]
    return total, shifted


def decay_block(zd, rate, bias, heads, lower):
    x = zd + bias
    soft = jnp.maximum(x, 0.0) + jnp.log1p(jnp.exp(-jnp.abs(x)))
    decay = rate * soft
    total = mm(lower, decay, NN, 6)
    beta = sigmoid(zd)
    return x, decay, total, beta


def inverse_unit_lower(systems, row, col):
    eye = jnp.where(row == col, 1.0, 0.0)
    out = None
    size = 1
    while size < BLOCK:
        pick = ((row ^ col) < 2 * size) & ((row & size) > 0) & ((col & size) == 0)
        level = [jnp.where(pick, a, 0.0) for a in systems]
        if out is None:
            out = [eye - l for l in level]
        else:
            inner = [mm(x, l, NN, PASS["inv"]) for x, l in zip(out, level)]
            out = [x - mm(i, x, NN, PASS["inv"]) for x, i in zip(out, inner)]
        size *= 2
    return out


def prepare(z_ext, zd, taps, rate, bias, live, heads, row, col):
    width = heads * HEAD_DIM
    lower = jnp.where(row >= col, 1.0, 0.0)
    conv, shifted = conv_block(z_ext, taps, live)
    gate = sigmoid(conv)
    mixed = conv * gate
    x, decay, total, beta = decay_block(zd, rate, bias, heads, lower)
    total_rows = total.T
    parts = []
    for h in range(heads):
        at = h * HEAD_DIM
        mq = mixed[:, at : at + HEAD_DIM]
        mk = mixed[:, width + at : width + at + HEAD_DIM]
        v = mixed[:, 2 * width + at : 2 * width + at + HEAD_DIM]
        rq = lax.rsqrt(lane_sum(mq * mq) + epsilon)
        rk = lax.rsqrt(lane_sum(mk * mk) + epsilon)
        qn = mq * rq
        k = mk * rk
        q = qn * HEAD_DIM**-0.5
        g = total[:, h : h + 1]
        g_row = total_rows[h : h + 1, :]
        g_last = total[BLOCK - 1 : BLOCK, h : h + 1]
        b = beta[:, heads + h : heads + h + 1]
        spread = jnp.exp(jnp.where(row >= col, g - g_row, -1e30))
        eg = jnp.exp(g)
        trail = jnp.exp(g_last - g)
        parts.append(
            dict(q=q, qn=qn, k=k, v=v, rq=rq, rk=rk, g=g, b=b, eg=eg, trail=trail,
                 trail_row=jnp.exp(g_last - g_row), spread=spread, keep=jnp.exp(g_last))
        )
    return conv, gate, shifted, x, decay, beta, parts


def forward_kernel(
    per_step, heads, offsets_ref, lengths_ref, z_ref, taps_ref, rate_ref, bias_ref, gain_ref,
    gated_ref, o_ref, states_ref, newest_ref, inverse_ref, state, halo,
):
    step = pl.program_id(0)
    width = heads * HEAD_DIM

    @pl.when(step == 0)
    def _():
        state[...] = jnp.zeros_like(state)
        halo[...] = jnp.zeros_like(halo)

    row, col = square_masks()
    rate, bias = -jnp.exp(rate_ref[...]), bias_ref[...]
    taps = taps_ref[...]
    prepared = []
    for n in range(per_step):
        at = n * BLOCK
        live, fresh = block_flags(offsets_ref, lengths_ref, (step * per_step + n) * BLOCK)
        before = halo[...] if n == 0 else z_ref[at - 8 : at, : 3 * width]
        before = before * as_scale(live * (1 - fresh))
        z_ext = jnp.concatenate([before, z_ref[at : at + BLOCK, : 3 * width]], axis=0)
        zd = z_ref[at : at + BLOCK, 4 * width : 4 * width + 128]
        _, _, _, _, _, _, parts = prepare(
            z_ext, zd, taps, rate, bias, as_scale(live), heads, row, col
        )
        for p in parts:
            p["gram"] = mm(jnp.concatenate([p["q"], p["k"]], axis=0), p["k"], NT, PASS["gram"])
        systems = [
            jnp.where(row > col, p["b"] * p["gram"][BLOCK:] * p["spread"], 0.0) for p in parts
        ]
        inverses = inverse_unit_lower(systems, row, col)
        for p, x in zip(parts, inverses):
            right = jnp.concatenate([p["k"] * (p["b"] * p["eg"]), p["v"] * p["b"]], axis=1)
            p["solved"] = mm(x, right, NN, PASS["solve"])
            p["scores"] = p["gram"][:BLOCK] * p["spread"]
            p["inverse"] = x
        prepared.append((at, as_scale(1 - fresh), parts))
    for n, (at, keep_flag, parts) in enumerate(prepared):
        for h, p in enumerate(parts):
            lanes = slice(h * HEAD_DIM, (h + 1) * HEAD_DIM)
            entry = state[h] * keep_flag
            states_ref[n, h] = entry
            both = mm(
                jnp.concatenate([p["solved"][:, :HEAD_DIM], p["q"] * p["eg"]], axis=0),
                entry, NN, PASS["state"],
            )
            newest = p["solved"][:, HEAD_DIM:] - both[:BLOCK]
            state[h] = p["keep"] * entry + mm(p["k"] * p["trail"], newest, TN, PASS["state"])
            o = both[BLOCK:] + mm(p["scores"], newest, NN, PASS["out"])
            newest_ref[at : at + BLOCK, lanes] = newest
            o_ref[at : at + BLOCK, lanes] = o
            inverse_ref[n, h] = p["inverse"]
            inv = lax.rsqrt(lane_sum(o * o) * (1.0 / HEAD_DIM) + epsilon)
            zg = z_ref[at : at + BLOCK, 3 * width + h * HEAD_DIM : 3 * width + (h + 1) * HEAD_DIM]
            gated = o * inv * gain_ref[...] * (zg * sigmoid(zg))
            gated_ref[at : at + BLOCK, lanes] = gated.astype(gated_ref.dtype)
    last = per_step * BLOCK
    halo[...] = z_ref[last - 8 : last, : 3 * width]


def backward_kernel(
    per_step, heads, steps, offsets_ref, lengths_ref, z_ref, before_ref, taps_ref, rate_ref,
    bias_ref, gain_ref, dgated_ref, o_ref, states_ref, newest_ref, inverse_ref,
    dz_ref, dtaps_ref, dgain_ref, drate_ref, dbias_ref, dstate, dhalo, carried,
):
    index = pl.program_id(0)
    step = steps - 1 - index
    width = heads * HEAD_DIM

    @pl.when(index == 0)
    def _():
        dstate[...] = jnp.zeros_like(dstate)
        dhalo[...] = jnp.zeros_like(dhalo)
        carried[...] = jnp.zeros_like(carried)
        dtaps_ref[...] = jnp.zeros_like(dtaps_ref)
        dgain_ref[...] = jnp.zeros_like(dgain_ref)
        drate_ref[...] = jnp.zeros_like(drate_ref)
        dbias_ref[...] = jnp.zeros_like(dbias_ref)

    row, col = square_masks()
    upper = jnp.where(row <= col, 1.0, 0.0)
    lane = lax.broadcasted_iota(jnp.int32, (BLOCK, 128), 1)
    below = lax.broadcasted_iota(jnp.int32, (BLOCK, 1), 0) == BLOCK - 1
    rate, bias = -jnp.exp(rate_ref[...]), bias_ref[...]
    taps, gain = taps_ref[...], gain_ref[...]
    fold = lambda v: jnp.sum(v.reshape(BLOCK // 8, 8, v.shape[1]), axis=0)
    for n in reversed(range(per_step)):
        at = n * BLOCK
        live, fresh = block_flags(offsets_ref, lengths_ref, (step * per_step + n) * BLOCK)
        before = before_ref[:, : 3 * width] if n == 0 else z_ref[at - 8 : at, : 3 * width]
        before = before * as_scale(live * (1 - fresh))
        z_ext = jnp.concatenate([before, z_ref[at : at + BLOCK, : 3 * width]], axis=0)
        zd = z_ref[at : at + BLOCK, 4 * width : 4 * width + 128]
        conv, gate, shifted, x, decay, beta, parts = prepare(
            z_ext, zd, taps, rate, bias, as_scale(live), heads, row, col
        )
        flow = as_scale(1 - fresh)
        dtotal = jnp.zeros((BLOCK, 128), jnp.float32)
        dbeta = jnp.zeros((BLOCK, 128), jnp.float32)
        dgain = jnp.zeros((BLOCK, HEAD_DIM), jnp.float32)
        dmixed = [[], [], []]
        dgates = []
        for h, p in enumerate(parts):
            lanes = slice(h * HEAD_DIM, (h + 1) * HEAD_DIM)
            q, k, v, b, spread = p["q"], p["k"], p["v"], p["b"], p["spread"]
            o = o_ref[at : at + BLOCK, lanes]
            newest = newest_ref[at : at + BLOCK, lanes]
            zg = z_ref[at : at + BLOCK, 3 * width + h * HEAD_DIM : 3 * width + (h + 1) * HEAD_DIM]
            dgated = dgated_ref[at : at + BLOCK, lanes].astype(jnp.float32)
            inv = lax.rsqrt(lane_sum(o * o) * (1.0 / HEAD_DIM) + epsilon)
            normed = o * inv
            sg = sigmoid(zg)
            silu = zg * sg
            dgates.append(dgated * (normed * gain) * (sg * (1.0 + zg * (1.0 - sg))))
            dy = dgated * silu
            dgain = dgain + dy * normed
            dn = dy * gain
            do = inv * (dn - normed * (lane_sum(dn * normed) * (1.0 / HEAD_DIM)))

            gram = mm(jnp.concatenate([q, k], axis=0), k, NT, PASS["gram"])
            scores = gram[:BLOCK] * spread
            beta_k = b * p["eg"]
            right = jnp.concatenate([k * beta_k, v * b], axis=1)
            inverse = inverse_ref[n, h]
            solved = mm(inverse, right, NN, PASS["solve"])
            entry = states_ref[n, h]
            ds = dstate[h]
            k_trail = k * p["trail"]
            dnew = mm(scores, do, TN, PASS["back"]) + mm(k_trail, ds, NN, PASS["back"])
            both = jnp.concatenate([do, dnew], axis=0)
            q_decay = q * p["eg"]
            sides = jnp.concatenate([q_decay, -solved[:, :HEAD_DIM]], axis=0)
            dentry = p["keep"] * ds + mm(sides, both, TN, PASS["back"])
            dstate[h] = dentry * flow
            dexit = carried[h : h + 1, :1]
            carried[h : h + 1, :] = flow * jnp.broadcast_to(
                lane_sum(jnp.sum(dentry * entry, axis=0, keepdims=True)), (1, 128)
            )
            dboth = mm(both, entry, NT, PASS["back"])
            dq_decay, dw = dboth[:BLOCK], -dboth[BLOCK:]
            dk_trail = mm(newest, ds, NT, PASS["back"])
            dscores = mm(do, newest, NT, PASS["back"])
            dright = mm(inverse, jnp.concatenate([dw, dnew], axis=1), TN, PASS["back"])
            dsystem = -mm(dright, solved, NT, PASS["back"])
            dgram = jnp.concatenate(
                [dscores * spread, jnp.where(row > col, dsystem * (b * spread), 0.0)], axis=0
            )
            straight = mm(dgram, k, NN, PASS["back"])
            across = mm(dgram, jnp.concatenate([q, k], axis=0), TN, PASS["back"])
            dq = straight[:BLOCK] + dq_decay * p["eg"]
            dk = (
                straight[BLOCK:] + across + dright[:, :HEAD_DIM] * beta_k + dk_trail * p["trail"]
            )
            dv = dright[:, HEAD_DIM:] * b
            dtot = lane_sum(do * o - dv * v) + jnp.where(below, dexit, 0.0)
            dbet = lane_sum(dright * solved) * (1.0 - b)
            dtotal = jnp.where(lane == h, dtot, dtotal)
            dbeta = jnp.where(lane == heads + h, dbet, dbeta)
            dqn = dq * HEAD_DIM**-0.5
            dmixed[0].append(p["rq"] * (dqn - p["qn"] * lane_sum(p["qn"] * dqn)))
            dmixed[1].append(p["rk"] * (dk - k * lane_sum(k * dk)))
            dmixed[2].append(dv)
        dmix = jnp.concatenate(dmixed[0] + dmixed[1] + dmixed[2], axis=1)
        dconv = dmix * (gate * (1.0 + conv * (1.0 - gate)))
        after = dhalo[...]
        ext = jnp.concatenate([dconv * as_scale(live), after], axis=0)
        dz = taps[3:4] * dconv
        for d in (1, 2, 3):
            dz = dz + taps[3 - d : 4 - d] * ext[d : d + BLOCK]
        dhalo[...] = dconv[:8] * as_scale(live * (1 - fresh))
        for d in range(4):
            dtaps_ref[3 - d] += fold(dconv * shifted[d])
        ddecay = mm(upper, dtotal, NN, 6)
        slope = ddecay * rate * sigmoid(x)
        dzd = slope + dbeta
        drate_ref[...] += fold(ddecay * decay)
        dbias_ref[...] += fold(slope)
        dgain_ref[...] += fold(dgain)
        dz_ref[at : at + BLOCK, : 3 * width] = dz.astype(dz_ref.dtype)
        for h in range(heads):
            dz_ref[
                at : at + BLOCK, 3 * width + h * HEAD_DIM : 3 * width + (h + 1) * HEAD_DIM
            ] = dgates[h].astype(dz_ref.dtype)
        dz_ref[at : at + BLOCK, 4 * width : 4 * width + 128] = dzd.astype(dz_ref.dtype)


def pad_lanes(v):
    return jnp.pad(v, (0, 128 - v.shape[0]))[None, :]


def mixer_forward(z, offsets, lengths, taps, decay_log, decay_bias, gain, per_step=2):
    rows, cols = z.shape
    heads = decay_log.shape[0]
    width = heads * HEAD_DIM
    blocks = rows // BLOCK
    steps = blocks // per_step
    tile = per_step * BLOCK
    smem = pl.BlockSpec(memory_space=pltpu.SMEM)
    whole = lambda shape: pl.BlockSpec(shape, lambda i: (0,) * len(shape))
    f32 = jnp.float32
    return pl.pallas_call(
        functools.partial(forward_kernel, per_step, heads),
        grid=(steps,),
        in_specs=[
            smem, smem,
            pl.BlockSpec((tile, cols), lambda i: (i, 0)),
            whole((4, 3 * width)), whole((1, 128)), whole((1, 128)), whole((1, HEAD_DIM)),
        ],
        out_specs=[
            pl.BlockSpec((tile, width), lambda i: (i, 0)),
            pl.BlockSpec((tile, width), lambda i: (i, 0)),
            pl.BlockSpec((per_step, heads, HEAD_DIM, HEAD_DIM), lambda i: (i, 0, 0, 0)),
            pl.BlockSpec((tile, width), lambda i: (i, 0)),
            pl.BlockSpec((per_step, heads, BLOCK, BLOCK), lambda i: (i, 0, 0, 0)),
        ],
        out_shape=[
            jax.ShapeDtypeStruct((rows, width), jnp.bfloat16),
            jax.ShapeDtypeStruct((rows, width), f32),
            jax.ShapeDtypeStruct((blocks, heads, HEAD_DIM, HEAD_DIM), f32),
            jax.ShapeDtypeStruct((rows, width), f32),
            jax.ShapeDtypeStruct((blocks, heads, BLOCK, BLOCK), f32),
        ],
        scratch_shapes=[
            pltpu.VMEM((heads, HEAD_DIM, HEAD_DIM), f32),
            pltpu.VMEM((8, 3 * width), f32),
        ],
        compiler_params=pltpu.CompilerParams(
            dimension_semantics=("arbitrary",), vmem_limit_bytes=48 * 1024 * 1024
        ),
        name="mixer_forward",
    )(offsets, lengths, z, taps, pad_lanes(decay_log), pad_lanes(decay_bias), gain[None, :])


def mixer_backward(
    z, offsets, lengths, taps, decay_log, decay_bias, gain, dgated, o, states, newest, inverses,
    per_step=2,
):
    rows, cols = z.shape
    heads = decay_log.shape[0]
    width = heads * HEAD_DIM
    blocks = rows // BLOCK
    steps = blocks // per_step
    tile = per_step * BLOCK
    smem = pl.BlockSpec(memory_space=pltpu.SMEM)
    whole = lambda shape: pl.BlockSpec(shape, lambda i: (0,) * len(shape))
    f32 = jnp.float32
    back = lambda i: (steps - 1 - i, 0)
    back4 = lambda i: (steps - 1 - i, 0, 0, 0)
    dz, dtaps, dgain, drate, dbias = pl.pallas_call(
        functools.partial(backward_kernel, per_step, heads, steps),
        grid=(steps,),
        in_specs=[
            smem, smem,
            pl.BlockSpec((tile, cols), back),
            pl.BlockSpec(
                (8, 3 * width), lambda i: (jnp.maximum((steps - 1 - i) * (tile // 8) - 1, 0), 0)
            ),
            whole((4, 3 * width)), whole((1, 128)), whole((1, 128)), whole((1, HEAD_DIM)),
            pl.BlockSpec((tile, width), back),
            pl.BlockSpec((tile, width), back),
            pl.BlockSpec((per_step, heads, HEAD_DIM, HEAD_DIM), back4),
            pl.BlockSpec((tile, width), back),
            pl.BlockSpec((per_step, heads, BLOCK, BLOCK), back4),
        ],
        out_specs=[
            pl.BlockSpec((tile, cols), back),
            whole((4, 8, 3 * width)), whole((8, HEAD_DIM)), whole((8, 128)), whole((8, 128)),
        ],
        out_shape=[
            jax.ShapeDtypeStruct((rows, cols), jnp.bfloat16),
            jax.ShapeDtypeStruct((4, 8, 3 * width), f32),
            jax.ShapeDtypeStruct((8, HEAD_DIM), f32),
            jax.ShapeDtypeStruct((8, 128), f32),
            jax.ShapeDtypeStruct((8, 128), f32),
        ],
        scratch_shapes=[
            pltpu.VMEM((heads, HEAD_DIM, HEAD_DIM), f32),
            pltpu.VMEM((8, 3 * width), f32),
            pltpu.VMEM((8, 128), f32),
        ],
        compiler_params=pltpu.CompilerParams(
            dimension_semantics=("arbitrary",), vmem_limit_bytes=48 * 1024 * 1024
        ),
        name="mixer_backward",
    )(
        offsets, lengths, z, z, taps, pad_lanes(decay_log), pad_lanes(decay_bias), gain[None, :],
        dgated, o, states, newest, inverses,
    )
    return (
        dz,
        jnp.sum(dtaps, axis=1),
        jnp.sum(dgain, axis=0),
        jnp.sum(drate, axis=0)[:heads],
        jnp.sum(dbias, axis=0)[:heads],
    )


def live_mask(offsets, lengths, total):
    positions = jnp.arange(total, dtype=jnp.int32)[:, None]
    inside = (positions >= offsets[None, :]) & (positions < offsets[None, :] + lengths[None, :])
    return jnp.any(inside, axis=1)


def project_rows(left, weight):
    return lax.dot_general(
        left, weight, (((1,), (1,)), ((), ())), preferred_element_type=jnp.float32
    )


def norm_back(grad_normed, base, inverse, gain):
    scaled = base * inverse
    gain_grad = jnp.sum(grad_normed * scaled, axis=0)
    inner = grad_normed * gain
    base_grad = inverse * (inner - scaled * jnp.mean(inner * scaled, axis=-1, keepdims=True))
    return (base_grad, gain_grad)


def gather_weight(weight):
    rows, columns = weight.shape
    shares = lax.all_gather(weight.astype(jnp.bfloat16), ("dp", "tensor"), axis=0, tiled=False)
    shares = shares.reshape(-1, lax.axis_size("tensor"), rows, columns)
    return jnp.transpose(shares, (0, 2, 1, 3)).reshape(shares.shape[0] * rows, -1)


def scatter_rows(left, right):
    part = lax.dot_general(
        left, right, (((0,), (0,)), ((), ())), preferred_element_type=jnp.float32
    )
    return lax.psum_scatter(part.astype(jnp.bfloat16), "dp", scatter_dimension=0, tiled=True)


def per_device(
    inputs,
    seq_offsets,
    seq_lengths,
    norm1_gain,
    w_qkv,
    w_gate_out,
    w_decay,
    conv_weight,
    decay_log,
    decay_bias,
    head_norm_gain,
    w_output,
    norm2_gain,
    w_mlp_in,
    w_mlp_out,
    cotangent,
):
    depth, width, heads = w_qkv.shape[0], w_qkv.shape[2], w_decay.shape[2]
    hidden_width = w_mlp_out.shape[1]
    low = jnp.bfloat16
    joined = jnp.concatenate(
        [
            w_qkv.reshape(depth, 3 * width),
            w_gate_out,
            w_decay.reshape(depth, 2 * heads),
            jnp.zeros((depth, 128 - 2 * heads), jnp.float32),
        ],
        axis=1,
    ).astype(low)
    stream = inputs.astype(jnp.float32)
    rows = stream.shape[0]
    scale_first = lax.rsqrt(jnp.mean(stream * stream, axis=-1, keepdims=True) + epsilon)
    normed_first = (stream * scale_first * norm1_gain).astype(low)
    mixer_full = lax.all_gather(joined, "dp", axis=0, tiled=True)
    first_all = lax.all_gather(normed_first, "tensor", axis=0, tiled=True)
    out_full = gather_weight(w_output)
    gate_full = gather_weight(w_mlp_in[:, 0])
    up_full = gather_weight(w_mlp_in[:, 1])
    down_full = gather_weight(w_mlp_out)
    total = first_all.shape[0]
    live_rows = live_mask(seq_offsets[0], seq_lengths[0], total)
    live_local = lax.dynamic_slice_in_dim(
        live_rows, lax.axis_index("tensor") * rows, rows, 0
    ).astype(jnp.float32)
    z = jnp.dot(first_all, mixer_full, preferred_element_type=jnp.float32)
    taps = jnp.transpose(conv_weight, (1, 0, 2)).reshape(4, 3 * width)
    gated_heads, mixed_out, states, newest, inverses = mixer_forward(
        z, seq_offsets, seq_lengths, taps, decay_log, decay_bias, head_norm_gain
    )
    gated = lax.all_to_all(gated_heads, "tensor", 0, 1, tiled=True)
    middle = stream + project_rows(gated, out_full)
    scale_second = lax.rsqrt(jnp.mean(middle * middle, axis=-1, keepdims=True) + epsilon)
    normed_second = (middle * scale_second * norm2_gain).astype(low)
    grad_out = cotangent.astype(jnp.float32) * live_local[:, None]
    grad_feed = grad_out.astype(low)
    gate_part = jnp.dot(normed_second, gate_full, preferred_element_type=jnp.float32)
    up_part = jnp.dot(normed_second, up_full, preferred_element_type=jnp.float32)
    sigma_gate = jax.nn.sigmoid(gate_part)
    silu_gate = gate_part * sigma_gate
    hidden = (silu_gate * up_part).astype(low)
    grad_hidden = jnp.dot(grad_feed, down_full, preferred_element_type=jnp.float32)
    grad_gate = (
        grad_hidden * up_part * sigma_gate * (1.0 + gate_part * (1.0 - sigma_gate))
    ).astype(low)
    grad_up = (grad_hidden * silu_gate).astype(low)
    grad_second = project_rows(grad_gate, gate_full) + project_rows(grad_up, up_full)
    grad_middle_norm, gain_second_part = norm_back(grad_second, middle, scale_second, norm2_gain)
    grad_middle = grad_out + grad_middle_norm
    grad_mixer = grad_middle.astype(low)
    grad_gated = lax.all_to_all(
        jnp.dot(grad_mixer, out_full, preferred_element_type=jnp.float32).astype(low),
        "tensor", 1, 0, tiled=True,
    )
    down_part = scatter_rows(grad_feed, hidden)
    gate_weight_part = scatter_rows(normed_second, grad_gate)
    up_weight_part = scatter_rows(normed_second, grad_up)
    out_part = scatter_rows(grad_mixer, gated)
    feed = project_rows(hidden, down_full)
    output = (live_local[:, None] * (middle + feed)).astype(low)
    grad_z, grad_taps, grad_head_gain, grad_log_rate, grad_rate_bias = mixer_backward(
        z, seq_offsets, seq_lengths, taps, decay_log, decay_bias, head_norm_gain,
        grad_gated, mixed_out, states, newest, inverses,
    )
    grad_kernel = jnp.transpose(grad_taps.reshape(4, 3, width), (1, 0, 2))
    shares = jnp.concatenate(
        [
            part.reshape(depth, -1, size)
            for part, size in (
                (gate_weight_part, hidden_width), (up_weight_part, hidden_width),
                (down_part, hidden_width), (out_part, width),
            )
        ],
        axis=2,
    )
    shares = lax.psum_scatter(shares, "tensor", scatter_dimension=1, tiled=True)
    shares = shares.reshape(depth, 3 * hidden_width + width).astype(jnp.float32)
    mlp_in_grad = shares[:, : 2 * hidden_width].reshape(depth, 2, hidden_width)
    mlp_out_grad = shares[:, 2 * hidden_width : 3 * hidden_width]
    output_grad = shares[:, 3 * hidden_width :]
    grad_first = lax.psum_scatter(
        project_rows(grad_z, mixer_full).astype(low), "tensor", scatter_dimension=0, tiled=True
    ).astype(jnp.float32)
    joined_grad = scatter_rows(first_all, grad_z).astype(jnp.float32)
    qkv_grad = joined_grad[:, : 3 * width].reshape(depth, 3, width)
    gate_grad = joined_grad[:, 3 * width : 4 * width]
    decay_grad = joined_grad[:, 4 * width : 4 * width + 2 * heads].reshape(depth, 2, heads)
    grad_stream_norm, gain_first_part = norm_back(grad_first, stream, scale_first, norm1_gain)
    grad_inputs = grad_middle + grad_stream_norm
    kernel_grad, log_rate_grad, rate_bias_grad = lax.psum(
        (grad_kernel, grad_log_rate, grad_rate_bias), "dp"
    )
    gain_first_grad, gain_second_grad, head_gain_grad = lax.psum(
        (gain_first_part, gain_second_part, grad_head_gain), ("dp", "tensor")
    )
    return (
        output,
        grad_inputs,
        gain_first_grad,
        qkv_grad,
        gate_grad,
        decay_grad,
        kernel_grad,
        log_rate_grad,
        rate_bias_grad,
        head_gain_grad,
        output_grad,
        gain_second_grad,
        mlp_in_grad,
        mlp_out_grad,
    )


def solution(mesh):
    placed = (
        P(("dp", "tensor"), None),
        P("dp", None),
        P("dp", None),
        P(),
        P("dp", None, "tensor"),
        P("dp", "tensor"),
        P("dp", None, "tensor"),
        P(None, None, "tensor"),
        P("tensor"),
        P("tensor"),
        P(),
        P("dp", "tensor"),
        P(),
        P("dp", None, "tensor"),
        P("dp", "tensor"),
        P(("dp", "tensor"), None),
    )
    return jax.shard_map(
        per_device,
        mesh=mesh,
        in_specs=placed,
        out_specs=(
            P(("dp", "tensor"), None),
            P(("dp", "tensor"), None),
            P(),
            P("dp", None, "tensor"),
            P("dp", "tensor"),
            P("dp", None, "tensor"),
            P(None, None, "tensor"),
            P("tensor"),
            P("tensor"),
            P(),
            P("dp", "tensor"),
            P(),
            P("dp", None, "tensor"),
            P("dp", "tensor"),
        ),
        check_vma=False,
    )
```

```python
import functools

import jax
import jax.numpy as jnp
from jax import lax
from jax.experimental import pallas as pl
from jax.experimental.pallas import tpu as pltpu
from jax.sharding import PartitionSpec as P

HEAD_DIM = 128
BLOCK = 64
epsilon = 1e-06
top_precision = lax.Precision.HIGHEST

NN = ((1,), (0,))
NT = ((1,), (1,))
TN = ((0,), (0,))


def mm(a, b, dims=NN, passes=1):
    if passes == 6:
        return lax.dot_general(
            a, b, (dims, ((), ())), precision=top_precision, preferred_element_type=jnp.float32
        )
    ah, bh = a.astype(jnp.bfloat16), b.astype(jnp.bfloat16)
    dot = lambda x, y: lax.dot_general(
        x, y, (dims, ((), ())), preferred_element_type=jnp.float32
    )
    total = dot(ah, bh)
    if passes == 3:
        al = (a - ah.astype(jnp.float32)).astype(jnp.bfloat16)
        bl = (b - bh.astype(jnp.float32)).astype(jnp.bfloat16)
        total = total + (dot(al, bh) + dot(ah, bl))
    return total


PASS = dict(gram=3, inv=3, solve=3, state=3, out=3, back=3)


def sigmoid(v):
    return 1.0 / (1.0 + jnp.exp(-v))


def lane_sum(v):
    return jnp.sum(v, axis=-1, keepdims=True)


def block_flags(offsets_ref, lengths_ref, start):
    live = jnp.int32(0)
    fresh = jnp.int32(0)
    for slot in range(offsets_ref.shape[1]):
        first, size = offsets_ref[0, slot], lengths_ref[0, slot]
        live = live | ((start >= first) & (start < first + size)).astype(jnp.int32)
        fresh = fresh | ((start == first) & (size > 0)).astype(jnp.int32)
    return live, fresh


def as_scale(flag):
    return jnp.where(flag > 0, 1.0, 0.0).astype(jnp.float32)


def square_masks():
    row = lax.broadcasted_iota(jnp.int32, (BLOCK, BLOCK), 0)
    col = lax.broadcasted_iota(jnp.int32, (BLOCK, BLOCK), 1)
    return row, col


def conv_block(ext, taps, live):
    shifted = [ext[8:]] + [ext[8 - d : 8 - d + BLOCK] * live for d in (1, 2, 3)]
    total = taps[3:4] * shifted[0]
    for d in (1, 2, 3):
        total = total + taps[3 - d : 4 - d] * shifted[d]
    return total, shifted


def decay_block(zd, rate, bias, heads, lower):
    x = zd + bias
    soft = jnp.maximum(x, 0.0) + jnp.log1p(jnp.exp(-jnp.abs(x)))
    decay = rate * soft
    total = mm(lower, decay, NN, 6)
    beta = sigmoid(zd)
    return x, decay, total, beta


def inverse_unit_lower(systems, row, col):
    eye = jnp.where(row == col, 1.0, 0.0)
    out = None
    size = 1
    while size < BLOCK:
        pick = ((row ^ col) < 2 * size) & ((row & size) > 0) & ((col & size) == 0)
        level = [jnp.where(pick, a, 0.0) for a in systems]
        if out is None:
            out = [eye - l for l in level]
        else:
            inner = [mm(x, l, NN, PASS["inv"]) for x, l in zip(out, level)]
            out = [x - mm(i, x, NN, PASS["inv"]) for x, i in zip(out, inner)]
        size *= 2
    return out


def prepare(z_ext, zd, taps, rate, bias, live, heads, row, col):
    width = heads * HEAD_DIM
    lower = jnp.where(row >= col, 1.0, 0.0)
    conv, shifted = conv_block(z_ext, taps, live)
    gate = sigmoid(conv)
    mixed = conv * gate
    x, decay, total, beta = decay_block(zd, rate, bias, heads, lower)
    total_rows = total.T
    parts = []
    for h in range(heads):
        at = h * HEAD_DIM
        mq = mixed[:, at : at + HEAD_DIM]
        mk = mixed[:, width + at : width + at + HEAD_DIM]
        v = mixed[:, 2 * width + at : 2 * width + at + HEAD_DIM]
        rq = lax.rsqrt(lane_sum(mq * mq) + epsilon)
        rk = lax.rsqrt(lane_sum(mk * mk) + epsilon)
        qn = mq * rq
        k = mk * rk
        q = qn * HEAD_DIM**-0.5
        g = total[:, h : h + 1]
        g_row = total_rows[h : h + 1, :]
        g_last = total[BLOCK - 1 : BLOCK, h : h + 1]
        b = beta[:, heads + h : heads + h + 1]
        spread = jnp.exp(jnp.where(row >= col, g - g_row, -1e30))
        eg = jnp.exp(g)
        trail = jnp.exp(g_last - g)
        parts.append(
            dict(q=q, qn=qn, k=k, v=v, rq=rq, rk=rk, g=g, b=b, eg=eg, trail=trail,
                 trail_row=jnp.exp(g_last - g_row), spread=spread, keep=jnp.exp(g_last))
        )
    return conv, gate, shifted, x, decay, beta, parts


def forward_kernel(
    per_step, heads, first, offsets_ref, lengths_ref, z_ref, taps_ref, rate_ref, bias_ref,
    gain_ref, state_in, halo_in,
    gated_ref, o_ref, states_ref, newest_ref, inverse_ref, state, halo,
):
    step = first + pl.program_id(0)
    width = heads * HEAD_DIM

    @pl.when(pl.program_id(0) == 0)
    def _():
        state[...] = state_in[...]
        halo[...] = halo_in[...]

    row, col = square_masks()
    rate, bias = -jnp.exp(rate_ref[...]), bias_ref[...]
    taps = taps_ref[...]
    prepared = []
    for n in range(per_step):
        at = n * BLOCK
        live, fresh = block_flags(offsets_ref, lengths_ref, (step * per_step + n) * BLOCK)
        before = halo[...] if n == 0 else z_ref[at - 8 : at, : 3 * width]
        before = before * as_scale(live * (1 - fresh))
        z_ext = jnp.concatenate([before, z_ref[at : at + BLOCK, : 3 * width]], axis=0)
        zd = z_ref[at : at + BLOCK, 4 * width : 4 * width + 128]
        _, _, _, _, _, _, parts = prepare(
            z_ext, zd, taps, rate, bias, as_scale(live), heads, row, col
        )
        for p in parts:
            p["gram"] = mm(jnp.concatenate([p["q"], p["k"]], axis=0), p["k"], NT, PASS["gram"])
        systems = [
            jnp.where(row > col, p["b"] * p["gram"][BLOCK:] * p["spread"], 0.0) for p in parts
        ]
        inverses = inverse_unit_lower(systems, row, col)
        for p, x in zip(parts, inverses):
            right = jnp.concatenate([p["k"] * (p["b"] * p["eg"]), p["v"] * p["b"]], axis=1)
            p["solved"] = mm(x, right, NN, PASS["solve"])
            p["scores"] = p["gram"][:BLOCK] * p["spread"]
            p["inverse"] = x
        prepared.append((at, as_scale(1 - fresh), parts))
    for n, (at, keep_flag, parts) in enumerate(prepared):
        for h, p in enumerate(parts):
            lanes = slice(h * HEAD_DIM, (h + 1) * HEAD_DIM)
            entry = state[h] * keep_flag
            states_ref[n, h] = entry
            both = mm(
                jnp.concatenate([p["solved"][:, :HEAD_DIM], p["q"] * p["eg"]], axis=0),
                entry, NN, PASS["state"],
            )
            newest = p["solved"][:, HEAD_DIM:] - both[:BLOCK]
            state[h] = p["keep"] * entry + mm(p["k"] * p["trail"], newest, TN, PASS["state"])
            o = both[BLOCK:] + mm(p["scores"], newest, NN, PASS["out"])
            newest_ref[at : at + BLOCK, lanes] = newest
            o_ref[at : at + BLOCK, lanes] = o
            inverse_ref[n, h] = p["inverse"]
            inv = lax.rsqrt(lane_sum(o * o) * (1.0 / HEAD_DIM) + epsilon)
            zg = z_ref[at : at + BLOCK, 3 * width + h * HEAD_DIM : 3 * width + (h + 1) * HEAD_DIM]
            gated = o * inv * gain_ref[...] * (zg * sigmoid(zg))
            gated_ref[at : at + BLOCK, lanes] = gated.astype(gated_ref.dtype)
    last = per_step * BLOCK
    halo[...] = z_ref[last - 8 : last, : 3 * width]


def backward_kernel(
    per_step, heads, last, offsets_ref, lengths_ref, z_ref, before_ref, taps_ref, rate_ref,
    bias_ref, gain_ref, dgated_ref, o_ref, states_ref, newest_ref, inverse_ref, *refs,
):
    given, (dz_ref, *kept) = refs[:7], refs[7:]
    dstate, dhalo, carried, dtaps_ref, dgain_ref, drate_ref, dbias_ref = kept
    index = pl.program_id(0)
    step = last - index
    width = heads * HEAD_DIM

    @pl.when(index == 0)
    def _():
        for source, target in zip(given, kept):
            target[...] = source[...]

    row, col = square_masks()
    upper = jnp.where(row <= col, 1.0, 0.0)
    lane = lax.broadcasted_iota(jnp.int32, (BLOCK, 128), 1)
    below = lax.broadcasted_iota(jnp.int32, (BLOCK, 1), 0) == BLOCK - 1
    rate, bias = -jnp.exp(rate_ref[...]), bias_ref[...]
    taps, gain = taps_ref[...], gain_ref[...]
    fold = lambda v: jnp.sum(v.reshape(BLOCK // 8, 8, v.shape[1]), axis=0)
    for n in reversed(range(per_step)):
        at = n * BLOCK
        live, fresh = block_flags(offsets_ref, lengths_ref, (step * per_step + n) * BLOCK)
        before = before_ref[:, : 3 * width] if n == 0 else z_ref[at - 8 : at, : 3 * width]
        before = before * as_scale(live * (1 - fresh))
        z_ext = jnp.concatenate([before, z_ref[at : at + BLOCK, : 3 * width]], axis=0)
        zd = z_ref[at : at + BLOCK, 4 * width : 4 * width + 128]
        conv, gate, shifted, x, decay, beta, parts = prepare(
            z_ext, zd, taps, rate, bias, as_scale(live), heads, row, col
        )
        flow = as_scale(1 - fresh)
        dtotal = jnp.zeros((BLOCK, 128), jnp.float32)
        dbeta = jnp.zeros((BLOCK, 128), jnp.float32)
        dgain = jnp.zeros((BLOCK, HEAD_DIM), jnp.float32)
        dmixed = [[], [], []]
        dgates = []
        for h, p in enumerate(parts):
            lanes = slice(h * HEAD_DIM, (h + 1) * HEAD_DIM)
            q, k, v, b, spread = p["q"], p["k"], p["v"], p["b"], p["spread"]
            o = o_ref[at : at + BLOCK, lanes]
            newest = newest_ref[at : at + BLOCK, lanes]
            zg = z_ref[at : at + BLOCK, 3 * width + h * HEAD_DIM : 3 * width + (h + 1) * HEAD_DIM]
            dgated = dgated_ref[at : at + BLOCK, lanes].astype(jnp.float32)
            inv = lax.rsqrt(lane_sum(o * o) * (1.0 / HEAD_DIM) + epsilon)
            normed = o * inv
            sg = sigmoid(zg)
            silu = zg * sg
            dgates.append(dgated * (normed * gain) * (sg * (1.0 + zg * (1.0 - sg))))
            dy = dgated * silu
            dgain = dgain + dy * normed
            dn = dy * gain
            do = inv * (dn - normed * (lane_sum(dn * normed) * (1.0 / HEAD_DIM)))

            gram = mm(jnp.concatenate([q, k], axis=0), k, NT, PASS["gram"])
            scores = gram[:BLOCK] * spread
            beta_k = b * p["eg"]
            right = jnp.concatenate([k * beta_k, v * b], axis=1)
            inverse = inverse_ref[n, h]
            solved = mm(inverse, right, NN, PASS["solve"])
            entry = states_ref[n, h]
            ds = dstate[h]
            k_trail = k * p["trail"]
            dnew = mm(scores, do, TN, PASS["back"]) + mm(k_trail, ds, NN, PASS["back"])
            both = jnp.concatenate([do, dnew], axis=0)
            q_decay = q * p["eg"]
            sides = jnp.concatenate([q_decay, -solved[:, :HEAD_DIM]], axis=0)
            dentry = p["keep"] * ds + mm(sides, both, TN, PASS["back"])
            dstate[h] = dentry * flow
            dexit = carried[h : h + 1, :1]
            carried[h : h + 1, :] = flow * jnp.broadcast_to(
                lane_sum(jnp.sum(dentry * entry, axis=0, keepdims=True)), (1, 128)
            )
            dboth = mm(both, entry, NT, PASS["back"])
            dq_decay, dw = dboth[:BLOCK], -dboth[BLOCK:]
            dk_trail = mm(newest, ds, NT, PASS["back"])
            dscores = mm(do, newest, NT, PASS["back"])
            dright = mm(inverse, jnp.concatenate([dw, dnew], axis=1), TN, PASS["back"])
            dsystem = -mm(dright, solved, NT, PASS["back"])
            dgram = jnp.concatenate(
                [dscores * spread, jnp.where(row > col, dsystem * (b * spread), 0.0)], axis=0
            )
            straight = mm(dgram, k, NN, PASS["back"])
            across = mm(dgram, jnp.concatenate([q, k], axis=0), TN, PASS["back"])
            dq = straight[:BLOCK] + dq_decay * p["eg"]
            dk = (
                straight[BLOCK:] + across + dright[:, :HEAD_DIM] * beta_k + dk_trail * p["trail"]
            )
            dv = dright[:, HEAD_DIM:] * b
            dtot = lane_sum(do * o - dv * v) + jnp.where(below, dexit, 0.0)
            dbet = lane_sum(dright * solved) * (1.0 - b)
            dtotal = jnp.where(lane == h, dtot, dtotal)
            dbeta = jnp.where(lane == heads + h, dbet, dbeta)
            dqn = dq * HEAD_DIM**-0.5
            dmixed[0].append(p["rq"] * (dqn - p["qn"] * lane_sum(p["qn"] * dqn)))
            dmixed[1].append(p["rk"] * (dk - k * lane_sum(k * dk)))
            dmixed[2].append(dv)
        dmix = jnp.concatenate(dmixed[0] + dmixed[1] + dmixed[2], axis=1)
        dconv = dmix * (gate * (1.0 + conv * (1.0 - gate)))
        after = dhalo[...]
        ext = jnp.concatenate([dconv * as_scale(live), after], axis=0)
        dz = taps[3:4] * dconv
        for d in (1, 2, 3):
            dz = dz + taps[3 - d : 4 - d] * ext[d : d + BLOCK]
        dhalo[...] = dconv[:8] * as_scale(live * (1 - fresh))
        for d in range(4):
            dtaps_ref[3 - d] += fold(dconv * shifted[d])
        ddecay = mm(upper, dtotal, NN, 6)
        slope = ddecay * rate * sigmoid(x)
        dzd = slope + dbeta
        drate_ref[...] += fold(ddecay * decay)
        dbias_ref[...] += fold(slope)
        dgain_ref[...] += fold(dgain)
        dz_ref[at : at + BLOCK, : 3 * width] = dz.astype(dz_ref.dtype)
        for h in range(heads):
            dz_ref[
                at : at + BLOCK, 3 * width + h * HEAD_DIM : 3 * width + (h + 1) * HEAD_DIM
            ] = dgates[h].astype(dz_ref.dtype)
        dz_ref[at : at + BLOCK, 4 * width : 4 * width + 128] = dzd.astype(dz_ref.dtype)


def pad_lanes(v):
    return jnp.pad(v, (0, 128 - v.shape[0]))[None, :]


def forward_carry(heads):
    return (
        jnp.zeros((heads, HEAD_DIM, HEAD_DIM), jnp.float32),
        jnp.zeros((8, 3 * heads * HEAD_DIM), jnp.float32),
    )


def backward_carry(heads):
    wide = 3 * heads * HEAD_DIM
    shapes = (
        (heads, HEAD_DIM, HEAD_DIM), (8, wide), (8, 128),
        (4, 8, wide), (8, HEAD_DIM), (8, 128), (8, 128),
    )
    return tuple(jnp.zeros(shape, jnp.float32) for shape in shapes)


def whole_block(shape):
    return pl.BlockSpec(shape, lambda i: (0,) * len(shape))


def mixer_forward(z, offsets, lengths, params, carry, chunk, chunks, per_step=2):
    rows, cols = z.shape
    heads = carry[0].shape[0]
    width = heads * HEAD_DIM
    blocks = rows // BLOCK // chunks
    steps = blocks // per_step
    tile = per_step * BLOCK
    first = chunk * steps
    smem = pl.BlockSpec(memory_space=pltpu.SMEM)
    f32 = jnp.float32
    out_rows = rows // chunks
    out = pl.pallas_call(
        functools.partial(forward_kernel, per_step, heads, first),
        grid=(steps,),
        in_specs=[
            smem, smem,
            pl.BlockSpec((tile, cols), lambda i: (first + i, 0)),
            *[whole_block(p.shape) for p in params],
            *[whole_block(c.shape) for c in carry],
        ],
        out_specs=[
            pl.BlockSpec((tile, width), lambda i: (i, 0)),
            pl.BlockSpec((tile, width), lambda i: (i, 0)),
            pl.BlockSpec((per_step, heads, HEAD_DIM, HEAD_DIM), lambda i: (i, 0, 0, 0)),
            pl.BlockSpec((tile, width), lambda i: (i, 0)),
            pl.BlockSpec((per_step, heads, BLOCK, BLOCK), lambda i: (i, 0, 0, 0)),
            *[whole_block(c.shape) for c in carry],
        ],
        out_shape=[
            jax.ShapeDtypeStruct((out_rows, width), jnp.bfloat16),
            jax.ShapeDtypeStruct((out_rows, width), f32),
            jax.ShapeDtypeStruct((blocks, heads, HEAD_DIM, HEAD_DIM), f32),
            jax.ShapeDtypeStruct((out_rows, width), f32),
            jax.ShapeDtypeStruct((blocks, heads, BLOCK, BLOCK), f32),
            *[jax.ShapeDtypeStruct(c.shape, f32) for c in carry],
        ],
        compiler_params=pltpu.CompilerParams(
            dimension_semantics=("arbitrary",), vmem_limit_bytes=48 * 1024 * 1024
        ),
        name="mixer_forward",
    )(offsets, lengths, z, *params, *carry)
    return out[:5], out[5:]


def mixer_backward(
    z, offsets, lengths, params, dgated, saved, carry, chunk, chunks, per_step=2
):
    rows, cols = z.shape
    heads = carry[0].shape[0]
    width = heads * HEAD_DIM
    blocks = rows // BLOCK // chunks
    steps = blocks // per_step
    tile = per_step * BLOCK
    last = chunk * steps + steps - 1
    smem = pl.BlockSpec(memory_space=pltpu.SMEM)
    f32 = jnp.float32
    back = lambda i: (steps - 1 - i, 0)
    back4 = lambda i: (steps - 1 - i, 0, 0, 0)
    out = pl.pallas_call(
        functools.partial(backward_kernel, per_step, heads, last),
        grid=(steps,),
        in_specs=[
            smem, smem,
            pl.BlockSpec((tile, cols), lambda i: (last - i, 0)),
            pl.BlockSpec(
                (8, 3 * width), lambda i: (jnp.maximum((last - i) * (tile // 8) - 1, 0), 0)
            ),
            *[whole_block(p.shape) for p in params],
            pl.BlockSpec((tile, width), lambda i: (last - i, 0)),
            pl.BlockSpec((tile, width), back),
            pl.BlockSpec((per_step, heads, HEAD_DIM, HEAD_DIM), back4),
            pl.BlockSpec((tile, width), back),
            pl.BlockSpec((per_step, heads, BLOCK, BLOCK), back4),
            *[whole_block(c.shape) for c in carry],
        ],
        out_specs=[
            pl.BlockSpec((tile, cols), back),
            *[whole_block(c.shape) for c in carry],
        ],
        out_shape=[
            jax.ShapeDtypeStruct((rows // chunks, cols), jnp.bfloat16),
            *[jax.ShapeDtypeStruct(c.shape, f32) for c in carry],
        ],
        compiler_params=pltpu.CompilerParams(
            dimension_semantics=("arbitrary",), vmem_limit_bytes=48 * 1024 * 1024
        ),
        cost_estimate=pl.CostEstimate(
            flops=blocks * heads * 1_000_000_000, bytes_accessed=blocks * heads * 400_000,
            transcendentals=0,
        ),
        name="mixer_backward",
    )(offsets, lengths, z, z, *params, dgated, *saved, *carry)
    return out[0], tuple(out[1:])


def live_mask(offsets, lengths, total):
    positions = jnp.arange(total, dtype=jnp.int32)[:, None]
    inside = (positions >= offsets[None, :]) & (positions < offsets[None, :] + lengths[None, :])
    return jnp.any(inside, axis=1)


def project_rows(left, weight):
    return lax.dot_general(
        left, weight, (((1,), (1,)), ((), ())), preferred_element_type=jnp.float32
    )


def norm_back(grad_normed, base, inverse, gain):
    scaled = base * inverse
    gain_grad = jnp.sum(grad_normed * scaled, axis=0)
    inner = grad_normed * gain
    base_grad = inverse * (inner - scaled * jnp.mean(inner * scaled, axis=-1, keepdims=True))
    return (base_grad, gain_grad)


def swap_cores(value):
    size = lax.axis_size("dp")
    return lax.ppermute(value, "dp", [(i, i ^ 1) for i in range(size)])


def chip_groups():
    size = lax.axis_size("dp")
    return [list(range(core, size, 2)) for core in range(2)]


def shift_tensor(value, distance):
    size = lax.axis_size("tensor")
    return lax.ppermute(value, "tensor", [(i, (i + distance) % size) for i in range(size)])


def ring_gather(value):
    size, me = lax.axis_size("tensor"), lax.axis_index("tensor")
    shards = [(me, value)]
    for step in range(1, size):
        value = shift_tensor(value, 1)
        shards.append(((me + size - step) % size, value))
    return shards


def place(shards, out=None):
    if out is None:
        out = jnp.zeros((len(shards),) + shards[0][1].shape, shards[0][1].dtype)
    for owner, shard in shards:
        out = lax.dynamic_update_index_in_dim(out, shard, owner, 0)
    return out


def by_core(mine, other):
    first = lax.axis_index("dp") % 2 == 0
    return jnp.stack([jnp.where(first, mine, other), jnp.where(first, other, mine)])


def halves(whole):
    core, size = lax.axis_index("dp") % 2, whole.shape[0] // 2
    return (
        lax.dynamic_slice_in_dim(whole, core * size, size, 0),
        lax.dynamic_slice_in_dim(whole, (1 - core) * size, size, 0),
    )


def core_half_slots(shares):
    mine, other = halves(shares)
    slots = jnp.transpose(by_core(mine, swap_cores(other)), (0, 2, 1, 3))
    return slots.reshape(2 * slots.shape[1], -1)


def gather_chips(slots):
    return lax.all_gather(slots, "dp", axis=0, tiled=True, axis_index_groups=chip_groups())


def after(values, *events):
    tied = lax.optimization_barrier((values, events))
    return tied[0]


def sum_shares(shares):
    total = lax.psum_scatter(shares, "tensor", scatter_dimension=0, tiled=True)
    return total[0].astype(jnp.float32)


def scatter_chips(part):
    return lax.psum_scatter(
        part, "dp", scatter_dimension=0, tiled=True, axis_index_groups=chip_groups()
    )


def core_half_grad(part, columns):
    keep, send = halves(part)
    both = by_core(keep, swap_cores(send))
    both = jnp.transpose(both.reshape(2, keep.shape[0], -1, columns), (0, 2, 1, 3))
    return both.reshape(-1, keep.shape[0], columns)


def outer(left, right):
    return lax.dot_general(
        left, right, (((0,), (0,)), ((), ())), preferred_element_type=jnp.float32
    ).astype(jnp.bfloat16)


def to_rows(heads_part):
    size, me = lax.axis_size("tensor"), lax.axis_index("tensor")
    rows, width = heads_part.shape[0] // size, heads_part.shape[1]
    out = jnp.zeros((rows, size * width), heads_part.dtype)
    for distance in range(size):
        to, source = (me + distance) % size, (me + size - distance) % size
        piece = lax.dynamic_slice_in_dim(heads_part, to * rows, rows, 0)
        if distance:
            piece = shift_tensor(piece, distance)
        out = lax.dynamic_update_slice_in_dim(out, piece, source * width, 1)
    return out


def to_heads(rows_part):
    size, me = lax.axis_size("tensor"), lax.axis_index("tensor")
    rows, width = rows_part.shape[0], rows_part.shape[1] // size
    out = jnp.zeros((size * rows, width), rows_part.dtype)
    for distance in range(size):
        to, source = (me + distance) % size, (me + size - distance) % size
        piece = lax.dynamic_slice_in_dim(rows_part, to * width, width, 1)
        if distance:
            piece = shift_tensor(piece, distance)
        out = lax.dynamic_update_slice_in_dim(out, piece, source * rows, 0)
    return out


def ring_sum(terms):
    size, me = lax.axis_size("tensor"), lax.axis_index("tensor")
    total = None
    for step in range(1, size + 1):
        own = lax.dynamic_index_in_dim(terms, (me + size - step) % size, 0, keepdims=False)
        own = own.astype(jnp.float32)
        total = own if total is None else own + total.astype(jnp.float32)
        if step < size:
            total = shift_tensor(total.astype(jnp.bfloat16), 1)
    return total


def sum_all(value, axes):
    for axis in axes:
        size, reach = lax.axis_size(axis), 1
        while reach < size:
            value = value + lax.ppermute(value, axis, [(i, i ^ reach) for i in range(size)])
            reach *= 2
    return value


def per_device(
    inputs,
    seq_offsets,
    seq_lengths,
    norm1_gain,
    w_qkv,
    w_gate_out,
    w_decay,
    conv_weight,
    decay_log,
    decay_bias,
    head_norm_gain,
    w_output,
    norm2_gain,
    w_mlp_in,
    w_mlp_out,
    cotangent,
):
    depth, width, heads = w_qkv.shape[0], w_qkv.shape[2], w_decay.shape[2]
    hidden_width = w_mlp_out.shape[1]
    low = jnp.bfloat16
    joined = jnp.concatenate(
        [
            w_qkv.reshape(depth, 3 * width),
            w_gate_out,
            w_decay.reshape(depth, 2 * heads),
            jnp.zeros((depth, 128 - 2 * heads), jnp.float32),
        ],
        axis=1,
    ).astype(low)
    stream = inputs.astype(jnp.float32)
    rows = stream.shape[0]
    scale_first = lax.rsqrt(jnp.mean(stream * stream, axis=-1, keepdims=True) + epsilon)
    normed_first = (stream * scale_first * norm1_gain).astype(low)
    mixer_full = lax.all_gather(joined, "dp", axis=0, tiled=True)
    early = jnp.concatenate([w_mlp_in[:, 0], w_mlp_in[:, 1], w_output], axis=1).astype(low)
    late = w_mlp_out.astype(low)
    chunks = lax.axis_size("tensor")
    early_shares = place(ring_gather(early))
    z_room = jnp.zeros((chunks, rows, joined.shape[1]), jnp.float32)
    first_room = jnp.zeros((chunks,) + normed_first.shape, low)
    early_shares, z_room, first_room = lax.optimization_barrier((early_shares, z_room, first_room))
    me = lax.axis_index("tensor")
    gate_slots = core_half_slots(early_shares[:, :, :hidden_width])
    up_slots = core_half_slots(early_shares[:, :, hidden_width : 2 * hidden_width])
    out_slots = jnp.transpose(early_shares[:, :, 2 * hidden_width :], (1, 0, 2))
    out_slots = out_slots.reshape(depth, -1)
    moved = after(normed_first, early_shares)
    first_shards = [(me, moved)]
    for step in range(1, chunks):
        moved = shift_tensor(moved, 1)
        if step == 1:
            moved, gate_slots, up_slots, out_slots = lax.optimization_barrier(
                (moved, gate_slots, up_slots, out_slots)
            )
            out_full = lax.all_gather(out_slots, "dp", axis=0, tiled=True)
            gate_full, up_full = gather_chips(gate_slots), gather_chips(up_slots)
        if step == chunks - 1:
            moved, out_full = lax.optimization_barrier((moved, out_full))
        first_shards.append(((me + chunks - step) % chunks, moved))
    late_shards = [(me, after(late, moved))]
    first_all = place(first_shards, first_room).reshape(-1, stream.shape[1])
    z = place(
        [
            (owner, jnp.dot(shard, mixer_full, preferred_element_type=jnp.float32))
            for owner, shard in first_shards
        ],
        z_room,
    ).reshape(first_all.shape[0], -1)
    live_rows = live_mask(seq_offsets[0], seq_lengths[0], first_all.shape[0])
    live_local = lax.dynamic_slice_in_dim(live_rows, me * rows, rows, 0).astype(jnp.float32)
    taps = jnp.transpose(conv_weight, (1, 0, 2)).reshape(4, 3 * width)
    params = (taps, pad_lanes(decay_log), pad_lanes(decay_bias), head_norm_gain[None, :])
    carry, saved, gated_parts = forward_carry(heads), [], []
    for chunk in range(chunks):
        (gated_part, *kept), carry = mixer_forward(
            z, seq_offsets, seq_lengths, params, carry, chunk, chunks
        )
        gated_parts.append(gated_part)
        saved.append(kept)
        if chunk < chunks - 1:
            moved = shift_tensor(late_shards[-1][1], 1)
            carry, moved = lax.optimization_barrier((carry, moved))
            late_shards.append(((me + chunks - 1 - chunk) % chunks, moved))
        if chunk == 0:
            carry, gate_full = lax.optimization_barrier((carry, gate_full))
        if chunk == chunks - 2:
            down_slots = core_half_slots(place(late_shards))
            carry, down_slots, up_full = lax.optimization_barrier((carry, down_slots, up_full))
            down_full = gather_chips(down_slots)
    gated = to_rows(jnp.concatenate(gated_parts, axis=0))
    middle = stream + project_rows(gated, out_full)
    scale_second = lax.rsqrt(jnp.mean(middle * middle, axis=-1, keepdims=True) + epsilon)
    normed_second = (middle * scale_second * norm2_gain).astype(low)
    grad_out = cotangent.astype(jnp.float32) * live_local[:, None]
    grad_feed = grad_out.astype(low)
    second_pair = jnp.concatenate([normed_second, swap_cores(normed_second)], axis=0)
    feed_grad_pair = jnp.concatenate([grad_feed, swap_cores(grad_feed)], axis=0)
    gate_part = jnp.dot(second_pair, gate_full, preferred_element_type=jnp.float32)
    grad_hidden = jnp.dot(feed_grad_pair, down_full, preferred_element_type=jnp.float32)
    up_part = jnp.dot(
        after(second_pair, grad_hidden), up_full, preferred_element_type=jnp.float32
    )
    sigma_gate = jax.nn.sigmoid(gate_part)
    silu_gate = gate_part * sigma_gate
    hidden = (silu_gate * up_part).astype(low)
    grad_gate = (
        grad_hidden * up_part * sigma_gate * (1.0 + gate_part * (1.0 - sigma_gate))
    ).astype(low)
    grad_up = (grad_hidden * silu_gate).astype(low)

    def back_rows(at):
        return project_rows(grad_gate[at], gate_full) + project_rows(grad_up[at], up_full)

    theirs = swap_cores(back_rows(slice(rows, None)).astype(low))
    grad_second = back_rows(slice(0, rows)) + theirs.astype(jnp.float32)
    grad_middle_norm, gain_second_part = norm_back(grad_second, middle, scale_second, norm2_gain)
    grad_middle = grad_out + grad_middle_norm
    grad_mixer = grad_middle.astype(low)
    down_scattered = scatter_chips(outer(feed_grad_pair, hidden))
    grad_gated_rows = jnp.dot(grad_mixer, out_full, preferred_element_type=jnp.float32).astype(low)
    grad_gated = to_heads(grad_gated_rows)
    second_pair, feed_pair = after((second_pair, hidden), grad_gated_rows)
    gate_scattered = scatter_chips(outer(second_pair, grad_gate))
    up_scattered = scatter_chips(outer(second_pair, grad_up))
    carry, grad_z_parts, terms = backward_carry(heads), [], []
    for chunk in reversed(range(chunks)):
        grad_z_part, carry = mixer_backward(
            z, seq_offsets, seq_lengths, params, grad_gated, saved[chunk], carry, chunk, chunks
        )
        grad_z_parts.insert(0, grad_z_part)
        terms.insert(0, project_rows(grad_z_part, mixer_full).astype(low))
        extra = ()
        if chunk == chunks - 1:
            extra = core_half_grad(after(down_scattered, grad_z_part), hidden_width)
        if chunk == chunks - 2:
            extra = core_half_grad(after(gate_scattered, grad_z_part), hidden_width)
        if chunk == 1:
            extra = core_half_grad(after(up_scattered, grad_z_part), hidden_width)
        carry, terms, extra, grad_z_parts = lax.optimization_barrier(
            (carry, terms, extra, grad_z_parts)
        )
        if chunk == chunks - 1:
            down_shares = sum_shares(extra)
        if chunk == chunks - 2:
            gate_shares = sum_shares(extra)
        if chunk == 1:
            up_shares = sum_shares(extra)
            out_part = lax.psum_scatter(
                outer(after(grad_mixer, extra), gated), "dp", scatter_dimension=0, tiled=True
            )
    joined_part = outer(first_all, jnp.concatenate(grad_z_parts, axis=0))
    down_shares, gate_shares, up_shares, out_part = after(
        (down_shares, gate_shares, up_shares, out_part), joined_part
    )
    out_shares = sum_shares(jnp.transpose(out_part.reshape(depth, -1, width), (1, 0, 2)))
    joined_grad = lax.psum_scatter(
        joined_part, "dp", scatter_dimension=0, tiled=True
    ).astype(jnp.float32)
    grad_first = ring_sum(jnp.stack(terms))
    grad_taps, grad_head_gain, grad_log_rate, grad_rate_bias = (
        jnp.sum(value, axis=-2) for value in carry[3:]
    )
    mlp_out_grad, output_grad = down_shares, out_shares
    mlp_in_grad = jnp.stack([gate_shares, up_shares], axis=1)
    feed_pair, down_late = after((feed_pair, down_full), joined_part)
    their_feed = swap_cores(project_rows(feed_pair[rows:], down_late).astype(low))
    feed = project_rows(feed_pair[:rows], down_late) + their_feed.astype(jnp.float32)
    output = (live_local[:, None] * (middle + feed)).astype(low)
    qkv_grad = joined_grad[:, : 3 * width].reshape(depth, 3, width)
    gate_grad = joined_grad[:, 3 * width : 4 * width]
    decay_grad = joined_grad[:, 4 * width : 4 * width + 2 * heads].reshape(depth, 2, heads)
    grad_stream_norm, gain_first_part = norm_back(grad_first, stream, scale_first, norm1_gain)
    grad_inputs = grad_middle + grad_stream_norm
    small = jnp.concatenate(
        [
            gain_first_part, gain_second_part, grad_head_gain,
            grad_taps.reshape(-1), grad_log_rate[:heads], grad_rate_bias[:heads],
        ]
    )
    model, shared = gain_first_part.shape[0], 2 * gain_first_part.shape[0] + HEAD_DIM
    small = jnp.pad(small, (0, -small.shape[0] % 1024)).reshape(-1, 128)
    small = sum_all(small, ("dp",))
    gains = sum_all(small[: shared // 128], ("tensor",)).reshape(-1)
    gain_first_grad, gain_second_grad = gains[:model], gains[model : 2 * model]
    head_gain_grad = gains[2 * model :]
    small = small.reshape(-1)[shared:]
    kernel_grad = jnp.transpose(small[: 12 * width].reshape(4, 3, width), (1, 0, 2))
    log_rate_grad = small[12 * width : 12 * width + heads]
    rate_bias_grad = small[12 * width + heads : 12 * width + 2 * heads]
    return (
        output,
        grad_inputs,
        gain_first_grad,
        qkv_grad,
        gate_grad,
        decay_grad,
        kernel_grad,
        log_rate_grad,
        rate_bias_grad,
        head_gain_grad,
        output_grad,
        gain_second_grad,
        mlp_in_grad,
        mlp_out_grad,
    )


def solution(mesh):
    placed = (
        P(("dp", "tensor"), None),
        P("dp", None),
        P("dp", None),
        P(),
        P("dp", None, "tensor"),
        P("dp", "tensor"),
        P("dp", None, "tensor"),
        P(None, None, "tensor"),
        P("tensor"),
        P("tensor"),
        P(),
        P("dp", "tensor"),
        P(),
        P("dp", None, "tensor"),
        P("dp", "tensor"),
        P(("dp", "tensor"), None),
    )
    return jax.shard_map(
        per_device,
        mesh=mesh,
        in_specs=placed,
        out_specs=(
            P(("dp", "tensor"), None),
            P(("dp", "tensor"), None),
            P(),
            P("dp", None, "tensor"),
            P("dp", "tensor"),
            P("dp", None, "tensor"),
            P(None, None, "tensor"),
            P("tensor"),
            P("tensor"),
            P(),
            P("dp", "tensor"),
            P(),
            P("dp", None, "tensor"),
            P("dp", "tensor"),
        ),
        check_vma=False,
    )
```

```python
import functools

import jax
import jax.numpy as jnp
from jax import lax
from jax.experimental import pallas as pl
from jax.experimental.pallas import tpu as pltpu
from jax.sharding import PartitionSpec as P

HEAD_DIM = 128
BLOCK = 64
epsilon = 1e-06
top_precision = lax.Precision.HIGHEST

NN = ((1,), (0,))
NT = ((1,), (1,))
TN = ((0,), (0,))


def mm(a, b, dims=NN, passes=1):
    if passes == 6:
        return lax.dot_general(
            a, b, (dims, ((), ())), precision=top_precision, preferred_element_type=jnp.float32
        )
    ah, bh = a.astype(jnp.bfloat16), b.astype(jnp.bfloat16)
    dot = lambda x, y: lax.dot_general(
        x, y, (dims, ((), ())), preferred_element_type=jnp.float32
    )
    total = dot(ah, bh)
    if passes == 3:
        al = (a - ah.astype(jnp.float32)).astype(jnp.bfloat16)
        bl = (b - bh.astype(jnp.float32)).astype(jnp.bfloat16)
        total = total + (dot(al, bh) + dot(ah, bl))
    return total


PASS = dict(gram=3, inv=3, solve=3, state=3, out=3, back=3, side=1)


def sigmoid(v):
    return 1.0 / (1.0 + jnp.exp(-v))


def lane_sum(v):
    return jnp.sum(v, axis=-1, keepdims=True)


def block_flags(offsets_ref, lengths_ref, start):
    live = jnp.int32(0)
    fresh = jnp.int32(0)
    for slot in range(offsets_ref.shape[1]):
        first, size = offsets_ref[0, slot], lengths_ref[0, slot]
        live = live | ((start >= first) & (start < first + size)).astype(jnp.int32)
        fresh = fresh | ((start == first) & (size > 0)).astype(jnp.int32)
    return live, fresh


def as_scale(flag):
    return jnp.where(flag > 0, 1.0, 0.0).astype(jnp.float32)


def square_masks():
    row = lax.broadcasted_iota(jnp.int32, (BLOCK, BLOCK), 0)
    col = lax.broadcasted_iota(jnp.int32, (BLOCK, BLOCK), 1)
    return row, col


def conv_block(ext, taps, live):
    shifted = [ext[8:]] + [ext[8 - d : 8 - d + BLOCK] * live for d in (1, 2, 3)]
    total = taps[3:4] * shifted[0]
    for d in (1, 2, 3):
        total = total + taps[3 - d : 4 - d] * shifted[d]
    return total, shifted


def decay_block(zd, rate, bias, heads, lower):
    x = zd + bias
    soft = jnp.maximum(x, 0.0) + jnp.log1p(jnp.exp(-jnp.abs(x)))
    decay = rate * soft
    total = mm(lower, decay, NN, 6)
    beta = sigmoid(zd)
    return x, decay, total, beta


def inverse_unit_lower(systems, row, col):
    eye = jnp.where(row == col, 1.0, 0.0)
    out = None
    size = 1
    while size < BLOCK:
        pick = ((row ^ col) < 2 * size) & ((row & size) > 0) & ((col & size) == 0)
        level = [jnp.where(pick, a, 0.0) for a in systems]
        if out is None:
            out = [eye - l for l in level]
        else:
            inner = [mm(x, l, NN, PASS["inv"]) for x, l in zip(out, level)]
            out = [x - mm(i, x, NN, PASS["inv"]) for x, i in zip(out, inner)]
        size *= 2
    return out


def prepare(z_ext, zd, taps, rate, bias, live, heads, row, col):
    width = heads * HEAD_DIM
    lower = jnp.where(row >= col, 1.0, 0.0)
    conv, shifted = conv_block(z_ext, taps, live)
    gate = sigmoid(conv)
    mixed = conv * gate
    x, decay, total, beta = decay_block(zd, rate, bias, heads, lower)
    total_rows = total.T
    parts = []
    for h in range(heads):
        at = h * HEAD_DIM
        mq = mixed[:, at : at + HEAD_DIM]
        mk = mixed[:, width + at : width + at + HEAD_DIM]
        v = mixed[:, 2 * width + at : 2 * width + at + HEAD_DIM]
        rq = lax.rsqrt(lane_sum(mq * mq) + epsilon)
        rk = lax.rsqrt(lane_sum(mk * mk) + epsilon)
        qn = mq * rq
        k = mk * rk
        q = qn * HEAD_DIM**-0.5
        g = total[:, h : h + 1]
        g_row = total_rows[h : h + 1, :]
        g_last = total[BLOCK - 1 : BLOCK, h : h + 1]
        b = beta[:, heads + h : heads + h + 1]
        spread = jnp.exp(jnp.where(row >= col, g - g_row, -1e30))
        eg = jnp.exp(g)
        trail = jnp.exp(g_last - g)
        parts.append(
            dict(q=q, qn=qn, k=k, v=v, rq=rq, rk=rk, g=g, b=b, eg=eg, trail=trail,
                 trail_row=jnp.exp(g_last - g_row), spread=spread, keep=jnp.exp(g_last))
        )
    return conv, gate, shifted, x, decay, beta, parts


def forward_kernel(
    per_step, heads, first, offsets_ref, lengths_ref, z_ref, taps_ref, rate_ref, bias_ref,
    gain_ref, state_in, halo_in,
    gated_ref, o_ref, states_ref, newest_ref, inverse_ref, state, halo,
):
    step = first + pl.program_id(0)
    width = heads * HEAD_DIM

    @pl.when(pl.program_id(0) == 0)
    def _():
        state[...] = state_in[...]
        halo[...] = halo_in[...]

    row, col = square_masks()
    rate, bias = -jnp.exp(rate_ref[...]), bias_ref[...]
    taps = taps_ref[...]
    prepared = []
    for n in range(per_step):
        at = n * BLOCK
        live, fresh = block_flags(offsets_ref, lengths_ref, (step * per_step + n) * BLOCK)
        before = halo[...] if n == 0 else z_ref[at - 8 : at, : 3 * width]
        before = before * as_scale(live * (1 - fresh))
        z_ext = jnp.concatenate([before, z_ref[at : at + BLOCK, : 3 * width]], axis=0)
        zd = z_ref[at : at + BLOCK, 4 * width : 4 * width + 128]
        _, _, _, _, _, _, parts = prepare(
            z_ext, zd, taps, rate, bias, as_scale(live), heads, row, col
        )
        for p in parts:
            p["gram"] = mm(jnp.concatenate([p["q"], p["k"]], axis=0), p["k"], NT, PASS["gram"])
        systems = [
            jnp.where(row > col, p["b"] * p["gram"][BLOCK:] * p["spread"], 0.0) for p in parts
        ]
        inverses = inverse_unit_lower(systems, row, col)
        for p, x in zip(parts, inverses):
            right = jnp.concatenate([p["k"] * (p["b"] * p["eg"]), p["v"] * p["b"]], axis=1)
            p["solved"] = mm(x, right, NN, PASS["solve"])
            p["scores"] = p["gram"][:BLOCK] * p["spread"]
            p["inverse"] = x
        prepared.append((at, as_scale(1 - fresh), parts))
    for n, (at, keep_flag, parts) in enumerate(prepared):
        for h, p in enumerate(parts):
            lanes = slice(h * HEAD_DIM, (h + 1) * HEAD_DIM)
            entry = state[h] * keep_flag
            states_ref[n, h] = entry
            both = mm(
                jnp.concatenate([p["solved"][:, :HEAD_DIM], p["q"] * p["eg"]], axis=0),
                entry, NN, PASS["state"],
            )
            newest = p["solved"][:, HEAD_DIM:] - both[:BLOCK]
            state[h] = p["keep"] * entry + mm(p["k"] * p["trail"], newest, TN, PASS["state"])
            o = both[BLOCK:] + mm(p["scores"], newest, NN, PASS["out"])
            newest_ref[at : at + BLOCK, lanes] = newest
            o_ref[at : at + BLOCK, lanes] = o
            inverse_ref[n, h] = p["inverse"]
            inv = lax.rsqrt(lane_sum(o * o) * (1.0 / HEAD_DIM) + epsilon)
            zg = z_ref[at : at + BLOCK, 3 * width + h * HEAD_DIM : 3 * width + (h + 1) * HEAD_DIM]
            gated = o * inv * gain_ref[...] * (zg * sigmoid(zg))
            gated_ref[at : at + BLOCK, lanes] = gated.astype(gated_ref.dtype)
    last = per_step * BLOCK
    halo[...] = z_ref[last - 8 : last, : 3 * width]


def backward_kernel(
    per_step, heads, last, offsets_ref, lengths_ref, z_ref, before_ref, taps_ref, rate_ref,
    bias_ref, gain_ref, dgated_ref, o_ref, states_ref, newest_ref, inverse_ref, *refs,
):
    given, (dz_ref, *kept) = refs[:7], refs[7:]
    dstate, dhalo, carried, dtaps_ref, dgain_ref, drate_ref, dbias_ref = kept
    index = pl.program_id(0)
    step = last - index
    width = heads * HEAD_DIM

    @pl.when(index == 0)
    def _():
        for source, target in zip(given, kept):
            target[...] = source[...]

    row, col = square_masks()
    upper = jnp.where(row <= col, 1.0, 0.0)
    lane = lax.broadcasted_iota(jnp.int32, (BLOCK, 128), 1)
    below = lax.broadcasted_iota(jnp.int32, (BLOCK, 1), 0) == BLOCK - 1
    rate, bias = -jnp.exp(rate_ref[...]), bias_ref[...]
    taps, gain = taps_ref[...], gain_ref[...]
    fold = lambda v: jnp.sum(v.reshape(BLOCK // 8, 8, v.shape[1]), axis=0)
    for n in reversed(range(per_step)):
        at = n * BLOCK
        live, fresh = block_flags(offsets_ref, lengths_ref, (step * per_step + n) * BLOCK)
        before = before_ref[:, : 3 * width] if n == 0 else z_ref[at - 8 : at, : 3 * width]
        before = before * as_scale(live * (1 - fresh))
        z_ext = jnp.concatenate([before, z_ref[at : at + BLOCK, : 3 * width]], axis=0)
        zd = z_ref[at : at + BLOCK, 4 * width : 4 * width + 128]
        conv, gate, shifted, x, decay, beta, parts = prepare(
            z_ext, zd, taps, rate, bias, as_scale(live), heads, row, col
        )
        flow = as_scale(1 - fresh)
        dtotal = jnp.zeros((BLOCK, 128), jnp.float32)
        dbeta = jnp.zeros((BLOCK, 128), jnp.float32)
        dgain = jnp.zeros((BLOCK, HEAD_DIM), jnp.float32)
        dmixed = [[], [], []]
        dgates = []
        for h, p in enumerate(parts):
            lanes = slice(h * HEAD_DIM, (h + 1) * HEAD_DIM)
            q, k, v, b, spread = p["q"], p["k"], p["v"], p["b"], p["spread"]
            o = o_ref[at : at + BLOCK, lanes]
            newest = newest_ref[at : at + BLOCK, lanes]
            zg = z_ref[at : at + BLOCK, 3 * width + h * HEAD_DIM : 3 * width + (h + 1) * HEAD_DIM]
            dgated = dgated_ref[at : at + BLOCK, lanes].astype(jnp.float32)
            inv = lax.rsqrt(lane_sum(o * o) * (1.0 / HEAD_DIM) + epsilon)
            normed = o * inv
            sg = sigmoid(zg)
            silu = zg * sg
            dgates.append(dgated * (normed * gain) * (sg * (1.0 + zg * (1.0 - sg))))
            dy = dgated * silu
            dgain = dgain + dy * normed
            dn = dy * gain
            do = inv * (dn - normed * (lane_sum(dn * normed) * (1.0 / HEAD_DIM)))

            gram = mm(jnp.concatenate([q, k], axis=0), k, NT, PASS["gram"])
            scores = gram[:BLOCK] * spread
            beta_k = b * p["eg"]
            right = jnp.concatenate([k * beta_k, v * b], axis=1)
            inverse = inverse_ref[n, h]
            solved = mm(inverse, right, NN, PASS["solve"])
            entry = states_ref[n, h]
            ds = dstate[h]
            k_trail = k * p["trail"]
            dnew = mm(scores, do, TN, PASS["back"]) + mm(k_trail, ds, NN, PASS["back"])
            both = jnp.concatenate([do, dnew], axis=0)
            q_decay = q * p["eg"]
            sides = jnp.concatenate([q_decay, -solved[:, :HEAD_DIM]], axis=0)
            dentry = p["keep"] * ds + mm(sides, both, TN, PASS["back"])
            dstate[h] = dentry * flow
            dexit = carried[h : h + 1, :1]
            carried[h : h + 1, :] = flow * jnp.broadcast_to(
                lane_sum(jnp.sum(dentry * entry, axis=0, keepdims=True)), (1, 128)
            )
            dboth = mm(both, entry, NT, PASS["side"])
            dq_decay, dw = dboth[:BLOCK], -dboth[BLOCK:]
            dk_trail = mm(newest, ds, NT, PASS["side"])
            dscores = mm(do, newest, NT, PASS["side"])
            dright = mm(inverse, jnp.concatenate([dw, dnew], axis=1), TN, PASS["back"])
            dsystem = -mm(dright, solved, NT, PASS["side"])
            dgram = jnp.concatenate(
                [dscores * spread, jnp.where(row > col, dsystem * (b * spread), 0.0)], axis=0
            )
            straight = mm(dgram, k, NN, PASS["side"])
            across = mm(dgram, jnp.concatenate([q, k], axis=0), TN, PASS["side"])
            dq = straight[:BLOCK] + dq_decay * p["eg"]
            dk = (
                straight[BLOCK:] + across + dright[:, :HEAD_DIM] * beta_k + dk_trail * p["trail"]
            )
            dv = dright[:, HEAD_DIM:] * b
            dtot = lane_sum(do * o - dv * v) + jnp.where(below, dexit, 0.0)
            dbet = lane_sum(dright * solved) * (1.0 - b)
            dtotal = jnp.where(lane == h, dtot, dtotal)
            dbeta = jnp.where(lane == heads + h, dbet, dbeta)
            dqn = dq * HEAD_DIM**-0.5
            dmixed[0].append(p["rq"] * (dqn - p["qn"] * lane_sum(p["qn"] * dqn)))
            dmixed[1].append(p["rk"] * (dk - k * lane_sum(k * dk)))
            dmixed[2].append(dv)
        dmix = jnp.concatenate(dmixed[0] + dmixed[1] + dmixed[2], axis=1)
        dconv = dmix * (gate * (1.0 + conv * (1.0 - gate)))
        after = dhalo[...]
        ext = jnp.concatenate([dconv * as_scale(live), after], axis=0)
        dz = taps[3:4] * dconv
        for d in (1, 2, 3):
            dz = dz + taps[3 - d : 4 - d] * ext[d : d + BLOCK]
        dhalo[...] = dconv[:8] * as_scale(live * (1 - fresh))
        for d in range(4):
            dtaps_ref[3 - d] += fold(dconv * shifted[d])
        ddecay = mm(upper, dtotal, NN, 6)
        slope = ddecay * rate * sigmoid(x)
        dzd = slope + dbeta
        drate_ref[...] += fold(ddecay * decay)
        dbias_ref[...] += fold(slope)
        dgain_ref[...] += fold(dgain)
        dz_ref[at : at + BLOCK, : 3 * width] = dz.astype(dz_ref.dtype)
        for h in range(heads):
            dz_ref[
                at : at + BLOCK, 3 * width + h * HEAD_DIM : 3 * width + (h + 1) * HEAD_DIM
            ] = dgates[h].astype(dz_ref.dtype)
        dz_ref[at : at + BLOCK, 4 * width : 4 * width + 128] = dzd.astype(dz_ref.dtype)


def pad_lanes(v):
    return jnp.pad(v, (0, 128 - v.shape[0]))[None, :]


def forward_carry(heads):
    return (
        jnp.zeros((heads, HEAD_DIM, HEAD_DIM), jnp.float32),
        jnp.zeros((8, 3 * heads * HEAD_DIM), jnp.float32),
    )


def backward_carry(heads):
    wide = 3 * heads * HEAD_DIM
    shapes = (
        (heads, HEAD_DIM, HEAD_DIM), (8, wide), (8, 128),
        (4, 8, wide), (8, HEAD_DIM), (8, 128), (8, 128),
    )
    return tuple(jnp.zeros(shape, jnp.float32) for shape in shapes)


def whole_block(shape):
    return pl.BlockSpec(shape, lambda i: (0,) * len(shape))


def mixer_forward(z, offsets, lengths, params, carry, chunk, chunks):
    rows, cols = z.shape
    heads = carry[0].shape[0]
    width = heads * HEAD_DIM
    blocks = rows // BLOCK // chunks
    per_step = 4 if blocks % 4 == 0 else 2
    steps = blocks // per_step
    tile = per_step * BLOCK
    first = chunk * steps
    smem = pl.BlockSpec(memory_space=pltpu.SMEM)
    f32 = jnp.float32
    out_rows = rows // chunks
    out = pl.pallas_call(
        functools.partial(forward_kernel, per_step, heads, first),
        grid=(steps,),
        in_specs=[
            smem, smem,
            pl.BlockSpec((tile, cols), lambda i: (first + i, 0)),
            *[whole_block(p.shape) for p in params],
            *[whole_block(c.shape) for c in carry],
        ],
        out_specs=[
            pl.BlockSpec((tile, width), lambda i: (i, 0)),
            pl.BlockSpec((tile, width), lambda i: (i, 0)),
            pl.BlockSpec((per_step, heads, HEAD_DIM, HEAD_DIM), lambda i: (i, 0, 0, 0)),
            pl.BlockSpec((tile, width), lambda i: (i, 0)),
            pl.BlockSpec((per_step, heads, BLOCK, BLOCK), lambda i: (i, 0, 0, 0)),
            *[whole_block(c.shape) for c in carry],
        ],
        out_shape=[
            jax.ShapeDtypeStruct((out_rows, width), jnp.bfloat16),
            jax.ShapeDtypeStruct((out_rows, width), f32),
            jax.ShapeDtypeStruct((blocks, heads, HEAD_DIM, HEAD_DIM), f32),
            jax.ShapeDtypeStruct((out_rows, width), f32),
            jax.ShapeDtypeStruct((blocks, heads, BLOCK, BLOCK), f32),
            *[jax.ShapeDtypeStruct(c.shape, f32) for c in carry],
        ],
        compiler_params=pltpu.CompilerParams(
            dimension_semantics=("arbitrary",), vmem_limit_bytes=48 * 1024 * 1024
        ),
        name="mixer_forward",
    )(offsets, lengths, z, *params, *carry)
    return out[:5], out[5:]


def mixer_backward(
    z, offsets, lengths, params, dgated, saved, carry, chunk, chunks
):
    rows, cols = z.shape
    heads = carry[0].shape[0]
    width = heads * HEAD_DIM
    blocks = rows // BLOCK // chunks
    per_step = 4 if blocks % 4 == 0 else 2
    steps = blocks // per_step
    tile = per_step * BLOCK
    last = chunk * steps + steps - 1
    smem = pl.BlockSpec(memory_space=pltpu.SMEM)
    f32 = jnp.float32
    back = lambda i: (steps - 1 - i, 0)
    back4 = lambda i: (steps - 1 - i, 0, 0, 0)
    out = pl.pallas_call(
        functools.partial(backward_kernel, per_step, heads, last),
        grid=(steps,),
        in_specs=[
            smem, smem,
            pl.BlockSpec((tile, cols), lambda i: (last - i, 0)),
            pl.BlockSpec(
                (8, 3 * width), lambda i: (jnp.maximum((last - i) * (tile // 8) - 1, 0), 0)
            ),
            *[whole_block(p.shape) for p in params],
            pl.BlockSpec((tile, width), lambda i: (last - i, 0)),
            pl.BlockSpec((tile, width), back),
            pl.BlockSpec((per_step, heads, HEAD_DIM, HEAD_DIM), back4),
            pl.BlockSpec((tile, width), back),
            pl.BlockSpec((per_step, heads, BLOCK, BLOCK), back4),
            *[whole_block(c.shape) for c in carry],
        ],
        out_specs=[
            pl.BlockSpec((tile, cols), back),
            *[whole_block(c.shape) for c in carry],
        ],
        out_shape=[
            jax.ShapeDtypeStruct((rows // chunks, cols), jnp.bfloat16),
            *[jax.ShapeDtypeStruct(c.shape, f32) for c in carry],
        ],
        compiler_params=pltpu.CompilerParams(
            dimension_semantics=("arbitrary",), vmem_limit_bytes=48 * 1024 * 1024
        ),
        cost_estimate=pl.CostEstimate(
            flops=blocks * heads * 1_000_000_000, bytes_accessed=blocks * heads * 400_000,
            transcendentals=0,
        ),
        name="mixer_backward",
    )(offsets, lengths, z, z, *params, dgated, *saved, *carry)
    return out[0], tuple(out[1:])


def live_mask(offsets, lengths, total):
    positions = jnp.arange(total, dtype=jnp.int32)[:, None]
    inside = (positions >= offsets[None, :]) & (positions < offsets[None, :] + lengths[None, :])
    return jnp.any(inside, axis=1)


def project_rows(left, weight):
    return lax.dot_general(
        left, weight, (((1,), (1,)), ((), ())), preferred_element_type=jnp.float32
    )


def norm_back(grad_normed, base, inverse, gain):
    scaled = base * inverse
    gain_grad = jnp.sum(grad_normed * scaled, axis=0)
    inner = grad_normed * gain
    base_grad = inverse * (inner - scaled * jnp.mean(inner * scaled, axis=-1, keepdims=True))
    return (base_grad, gain_grad)


def swap_cores(value):
    size = lax.axis_size("dp")
    return lax.ppermute(value, "dp", [(i, i ^ 1) for i in range(size)])


def chip_groups():
    size = lax.axis_size("dp")
    return [list(range(core, size, 2)) for core in range(2)]


def shift_tensor(value, distance):
    size = lax.axis_size("tensor")
    return lax.ppermute(value, "tensor", [(i, (i + distance) % size) for i in range(size)])


def ring_gather(value):
    size, me = lax.axis_size("tensor"), lax.axis_index("tensor")
    shards = [(me, value)]
    for step in range(1, size):
        value = shift_tensor(value, 1)
        shards.append(((me + size - step) % size, value))
    return shards


def place(shards, out=None):
    if out is None:
        out = jnp.zeros((len(shards),) + shards[0][1].shape, shards[0][1].dtype)
    for owner, shard in shards:
        out = lax.dynamic_update_index_in_dim(out, shard, owner, 0)
    return out


def by_core(mine, other):
    first = lax.axis_index("dp") % 2 == 0
    return jnp.stack([jnp.where(first, mine, other), jnp.where(first, other, mine)])


def halves(whole):
    core, size = lax.axis_index("dp") % 2, whole.shape[0] // 2
    return (
        lax.dynamic_slice_in_dim(whole, core * size, size, 0),
        lax.dynamic_slice_in_dim(whole, (1 - core) * size, size, 0),
    )


def core_half_slots(shares):
    mine, other = halves(shares)
    slots = jnp.transpose(by_core(mine, swap_cores(other)), (0, 2, 1, 3))
    return slots.reshape(2 * slots.shape[1], -1)


def gather_chips(slots):
    return lax.all_gather(slots, "dp", axis=0, tiled=True, axis_index_groups=chip_groups())


def after(values, *events):
    tied = lax.optimization_barrier((values, events))
    return tied[0]


def sum_shares(shares):
    total = lax.psum_scatter(shares, "tensor", scatter_dimension=0, tiled=True)
    return total[0].astype(jnp.float32)


def scatter_chips(part):
    return lax.psum_scatter(
        part, "dp", scatter_dimension=0, tiled=True, axis_index_groups=chip_groups()
    )


def core_half_grad(part, columns):
    keep, send = halves(part)
    both = by_core(keep, swap_cores(send))
    both = jnp.transpose(both.reshape(2, keep.shape[0], -1, columns), (0, 2, 1, 3))
    return both.reshape(-1, keep.shape[0], columns)


def outer(left, right):
    return lax.dot_general(
        left, right, (((0,), (0,)), ((), ())), preferred_element_type=jnp.float32
    ).astype(jnp.bfloat16)


def to_rows(heads_part):
    size, me = lax.axis_size("tensor"), lax.axis_index("tensor")
    rows, width = heads_part.shape[0] // size, heads_part.shape[1]
    out = jnp.zeros((rows, size * width), heads_part.dtype)
    for distance in range(size):
        to, source = (me + distance) % size, (me + size - distance) % size
        piece = lax.dynamic_slice_in_dim(heads_part, to * rows, rows, 0)
        if distance:
            piece = shift_tensor(piece, distance)
        out = lax.dynamic_update_slice_in_dim(out, piece, source * width, 1)
    return out


def to_heads(rows_part):
    size, me = lax.axis_size("tensor"), lax.axis_index("tensor")
    rows, width = rows_part.shape[0], rows_part.shape[1] // size
    out = jnp.zeros((size * rows, width), rows_part.dtype)
    for distance in range(size):
        to, source = (me + distance) % size, (me + size - distance) % size
        piece = lax.dynamic_slice_in_dim(rows_part, to * width, width, 1)
        if distance:
            piece = shift_tensor(piece, distance)
        out = lax.dynamic_update_slice_in_dim(out, piece, source * rows, 0)
    return out


def ring_sum(terms):
    size, me = lax.axis_size("tensor"), lax.axis_index("tensor")
    total = None
    for step in range(1, size + 1):
        own = lax.dynamic_index_in_dim(terms, (me + size - step) % size, 0, keepdims=False)
        own = own.astype(jnp.float32)
        total = own if total is None else own + total.astype(jnp.float32)
        if step < size:
            total = shift_tensor(total.astype(jnp.bfloat16), 1)
    return total


def sum_all(value, axes):
    for axis in axes:
        size, reach = lax.axis_size(axis), 1
        while reach < size:
            value = value + lax.ppermute(value, axis, [(i, i ^ reach) for i in range(size)])
            reach *= 2
    return value


def per_device(
    inputs,
    seq_offsets,
    seq_lengths,
    norm1_gain,
    w_qkv,
    w_gate_out,
    w_decay,
    conv_weight,
    decay_log,
    decay_bias,
    head_norm_gain,
    w_output,
    norm2_gain,
    w_mlp_in,
    w_mlp_out,
    cotangent,
):
    depth, width, heads = w_qkv.shape[0], w_qkv.shape[2], w_decay.shape[2]
    hidden_width = w_mlp_out.shape[1]
    low = jnp.bfloat16
    joined = jnp.concatenate(
        [
            w_qkv.reshape(depth, 3 * width),
            w_gate_out,
            w_decay.reshape(depth, 2 * heads),
            jnp.zeros((depth, 128 - 2 * heads), jnp.float32),
        ],
        axis=1,
    ).astype(low)
    stream = inputs.astype(jnp.float32)
    rows = stream.shape[0]
    scale_first = lax.rsqrt(jnp.mean(stream * stream, axis=-1, keepdims=True) + epsilon)
    normed_first = (stream * scale_first * norm1_gain).astype(low)
    mixer_full = lax.all_gather(joined, "dp", axis=0, tiled=True)
    early = jnp.concatenate([w_mlp_in[:, 0], w_mlp_in[:, 1], w_output], axis=1).astype(low)
    late = w_mlp_out.astype(low)
    chunks = lax.axis_size("tensor")
    early_shares = place(ring_gather(early))
    z_room = jnp.zeros((chunks, rows, joined.shape[1]), jnp.float32)
    first_room = jnp.zeros((chunks,) + normed_first.shape, low)
    early_shares, z_room, first_room = lax.optimization_barrier((early_shares, z_room, first_room))
    me = lax.axis_index("tensor")
    gate_slots = core_half_slots(early_shares[:, :, :hidden_width])
    up_slots = core_half_slots(early_shares[:, :, hidden_width : 2 * hidden_width])
    out_slots = jnp.transpose(early_shares[:, :, 2 * hidden_width :], (1, 0, 2))
    out_slots = out_slots.reshape(depth, -1)
    moved = after(normed_first, early_shares)
    first_shards = [(me, moved)]
    for step in range(1, chunks):
        moved = shift_tensor(moved, 1)
        if step == 1:
            moved, gate_slots, up_slots, out_slots = lax.optimization_barrier(
                (moved, gate_slots, up_slots, out_slots)
            )
            out_full = lax.all_gather(out_slots, "dp", axis=0, tiled=True)
            gate_full, up_full = gather_chips(gate_slots), gather_chips(up_slots)
        if step == chunks - 1:
            moved, out_full = lax.optimization_barrier((moved, out_full))
        first_shards.append(((me + chunks - step) % chunks, moved))
    late_shards = [(me, after(late, moved))]
    first_all = place(first_shards, first_room).reshape(-1, stream.shape[1])
    z = place(
        [
            (owner, jnp.dot(shard, mixer_full, preferred_element_type=jnp.float32))
            for owner, shard in first_shards
        ],
        z_room,
    ).reshape(first_all.shape[0], -1)
    live_rows = live_mask(seq_offsets[0], seq_lengths[0], first_all.shape[0])
    live_local = lax.dynamic_slice_in_dim(live_rows, me * rows, rows, 0).astype(jnp.float32)
    taps = jnp.transpose(conv_weight, (1, 0, 2)).reshape(4, 3 * width)
    params = (taps, pad_lanes(decay_log), pad_lanes(decay_bias), head_norm_gain[None, :])
    carry, saved, gated_parts = forward_carry(heads), [], []
    for chunk in range(chunks):
        (gated_part, *kept), carry = mixer_forward(
            z, seq_offsets, seq_lengths, params, carry, chunk, chunks
        )
        gated_parts.append(gated_part)
        saved.append(kept)
        if chunk < chunks - 1:
            moved = shift_tensor(late_shards[-1][1], 1)
            carry, moved = lax.optimization_barrier((carry, moved))
            late_shards.append(((me + chunks - 1 - chunk) % chunks, moved))
        if chunk == 0:
            carry, gate_full = lax.optimization_barrier((carry, gate_full))
        if chunk == chunks - 2:
            down_slots = core_half_slots(place(late_shards))
            carry, down_slots, up_full = lax.optimization_barrier((carry, down_slots, up_full))
            down_full = gather_chips(down_slots)
    gated = to_rows(jnp.concatenate(gated_parts, axis=0))
    middle = stream + project_rows(gated, out_full)
    scale_second = lax.rsqrt(jnp.mean(middle * middle, axis=-1, keepdims=True) + epsilon)
    normed_second = (middle * scale_second * norm2_gain).astype(low)
    grad_out = cotangent.astype(jnp.float32) * live_local[:, None]
    grad_feed = grad_out.astype(low)
    second_pair = jnp.concatenate([normed_second, swap_cores(normed_second)], axis=0)
    feed_grad_pair = jnp.concatenate([grad_feed, swap_cores(grad_feed)], axis=0)
    gate_part = jnp.dot(second_pair, gate_full, preferred_element_type=jnp.float32)
    grad_hidden = jnp.dot(feed_grad_pair, down_full, preferred_element_type=jnp.float32)
    up_part = jnp.dot(
        after(second_pair, grad_hidden), up_full, preferred_element_type=jnp.float32
    )
    sigma_gate = jax.nn.sigmoid(gate_part)
    silu_gate = gate_part * sigma_gate
    hidden = (silu_gate * up_part).astype(low)
    grad_gate = (
        grad_hidden * up_part * sigma_gate * (1.0 + gate_part * (1.0 - sigma_gate))
    ).astype(low)
    grad_up = (grad_hidden * silu_gate).astype(low)

    def back_rows(at):
        return project_rows(grad_gate[at], gate_full) + project_rows(grad_up[at], up_full)

    theirs = swap_cores(back_rows(slice(rows, None)).astype(low))
    grad_second = back_rows(slice(0, rows)) + theirs.astype(jnp.float32)
    grad_middle_norm, gain_second_part = norm_back(grad_second, middle, scale_second, norm2_gain)
    grad_middle = grad_out + grad_middle_norm
    grad_mixer = grad_middle.astype(low)
    down_scattered = scatter_chips(outer(feed_grad_pair, hidden))
    grad_gated_rows = jnp.dot(grad_mixer, out_full, preferred_element_type=jnp.float32).astype(low)
    grad_gated = to_heads(grad_gated_rows)
    second_pair, feed_pair = after((second_pair, hidden), grad_gated_rows)
    gate_scattered = scatter_chips(outer(second_pair, grad_gate))
    up_scattered = scatter_chips(outer(second_pair, grad_up))
    carry, grad_z_parts, terms = backward_carry(heads), [], []
    for chunk in reversed(range(chunks)):
        grad_z_part, carry = mixer_backward(
            z, seq_offsets, seq_lengths, params, grad_gated, saved[chunk], carry, chunk, chunks
        )
        grad_z_parts.insert(0, grad_z_part)
        terms.insert(0, project_rows(grad_z_part, mixer_full).astype(low))
        extra = ()
        if chunk == chunks - 1:
            extra = core_half_grad(after(down_scattered, grad_z_part), hidden_width)
        if chunk == chunks - 2:
            extra = core_half_grad(after(gate_scattered, grad_z_part), hidden_width)
        if chunk == 1:
            extra = core_half_grad(after(up_scattered, grad_z_part), hidden_width)
        carry, terms, extra, grad_z_parts = lax.optimization_barrier(
            (carry, terms, extra, grad_z_parts)
        )
        if chunk == chunks - 1:
            down_shares = sum_shares(extra)
        if chunk == chunks - 2:
            gate_shares = sum_shares(extra)
        if chunk == 1:
            up_shares = sum_shares(extra)
            out_part = lax.psum_scatter(
                outer(after(grad_mixer, extra), gated), "dp", scatter_dimension=0, tiled=True
            )
    joined_part = outer(first_all, jnp.concatenate(grad_z_parts, axis=0))
    down_shares, gate_shares, up_shares, out_part = after(
        (down_shares, gate_shares, up_shares, out_part), joined_part
    )
    out_shares = sum_shares(jnp.transpose(out_part.reshape(depth, -1, width), (1, 0, 2)))
    joined_grad = lax.psum_scatter(
        joined_part, "dp", scatter_dimension=0, tiled=True
    ).astype(jnp.float32)
    grad_first = ring_sum(jnp.stack(terms))
    grad_taps, grad_head_gain, grad_log_rate, grad_rate_bias = (
        jnp.sum(value, axis=-2) for value in carry[3:]
    )
    mlp_out_grad, output_grad = down_shares, out_shares
    mlp_in_grad = jnp.stack([gate_shares, up_shares], axis=1)
    feed_pair, down_late = after((feed_pair, down_full), joined_part)
    their_feed = swap_cores(project_rows(feed_pair[rows:], down_late).astype(low))
    feed = project_rows(feed_pair[:rows], down_late) + their_feed.astype(jnp.float32)
    output = (live_local[:, None] * (middle + feed)).astype(low)
    qkv_grad = joined_grad[:, : 3 * width].reshape(depth, 3, width)
    gate_grad = joined_grad[:, 3 * width : 4 * width]
    decay_grad = joined_grad[:, 4 * width : 4 * width + 2 * heads].reshape(depth, 2, heads)
    grad_stream_norm, gain_first_part = norm_back(grad_first, stream, scale_first, norm1_gain)
    grad_inputs = grad_middle + grad_stream_norm
    small = jnp.concatenate(
        [
            gain_first_part, gain_second_part, grad_head_gain,
            grad_taps.reshape(-1), grad_log_rate[:heads], grad_rate_bias[:heads],
        ]
    )
    model, shared = gain_first_part.shape[0], 2 * gain_first_part.shape[0] + HEAD_DIM
    small = jnp.pad(small, (0, -small.shape[0] % 1024)).reshape(-1, 128)
    small = sum_all(small, ("dp",))
    gains = sum_all(small[: shared // 128], ("tensor",)).reshape(-1)
    gain_first_grad, gain_second_grad = gains[:model], gains[model : 2 * model]
    head_gain_grad = gains[2 * model :]
    small = small.reshape(-1)[shared:]
    kernel_grad = jnp.transpose(small[: 12 * width].reshape(4, 3, width), (1, 0, 2))
    log_rate_grad = small[12 * width : 12 * width + heads]
    rate_bias_grad = small[12 * width + heads : 12 * width + 2 * heads]
    return (
        output,
        grad_inputs,
        gain_first_grad,
        qkv_grad,
        gate_grad,
        decay_grad,
        kernel_grad,
        log_rate_grad,
        rate_bias_grad,
        head_gain_grad,
        output_grad,
        gain_second_grad,
        mlp_in_grad,
        mlp_out_grad,
    )


def solution(mesh):
    placed = (
        P(("dp", "tensor"), None),
        P("dp", None),
        P("dp", None),
        P(),
        P("dp", None, "tensor"),
        P("dp", "tensor"),
        P("dp", None, "tensor"),
        P(None, None, "tensor"),
        P("tensor"),
        P("tensor"),
        P(),
        P("dp", "tensor"),
        P(),
        P("dp", None, "tensor"),
        P("dp", "tensor"),
        P(("dp", "tensor"), None),
    )
    return jax.shard_map(
        per_device,
        mesh=mesh,
        in_specs=placed,
        out_specs=(
            P(("dp", "tensor"), None),
            P(("dp", "tensor"), None),
            P(),
            P("dp", None, "tensor"),
            P("dp", "tensor"),
            P("dp", None, "tensor"),
            P(None, None, "tensor"),
            P("tensor"),
            P("tensor"),
            P(),
            P("dp", "tensor"),
            P(),
            P("dp", None, "tensor"),
            P("dp", "tensor"),
        ),
        check_vma=False,
    )
```
